256 devices in a mesh: bucket: 32 (over y, z), col: 8 (over x, core).
Axes of the slice: x: 4, y: 4, z: 8, core: 2. Of those that a mesh axis runs over, the one named last changes fastest.
Arguments:
- entity_table: bfloat16 [262144, 1024], P('bucket', 'col'), may hold values from -9 to 9
- relation_table: bfloat16 [4096, 1024], P(None, 'col'), may hold values from -4 to 4
- head_row: int32 [65536], P('bucket'), may hold values from 0 to 8191
- relation_id: int32 [65536], P('bucket'), may hold values from 0 to 4095
- tail_owner: int32 [65536, 1], P('bucket'), may hold values from 0 to 31; in each aligned block of 2048 rows (0 to 2047, 2048 to 4095, ...) at most 128 rows name the same one
- tail_row: int32 [65536], P('bucket'), may hold values from 0 to 8191
- negative_row: int32 [128, 1000], P('bucket'), may hold values from 0 to 8191
Outputs:
- loss: float32 [65536], P('bucket')
- entity_grad: float32 [262144, 1024], P('bucket', 'col')
- relation_grad: float32 [4096, 1024], P('bucket', 'col')
The draws below stay inside these ranges and needn't reach their ends.
Inputs may be any that keep to these rules, and one draw needn't show every extreme that they name: `tail_owner`: in the 2048 edges of one bucket group no partition is named more than 128 times, a bound that some block reaches.
All inputs are finite; a program needn't handle non-finite values.
Results may differ from the reference program's by a relative error of at most 0.0061.
Values may be sent and summed in bfloat16 or wider, within the bound.
A program may use at most 64 MiB of HBM per device.

```python
import math
import jax
import jax.numpy as jnp
import numpy as np
from jax import lax

D = 1024
PAIR = 128
REL = 4096
NEG = 1000
SPAN = 512
ENT_DEV = 8192
EDGES_DEV = 2048
ENTITIES = 262144
EDGES = 65536
SPANS = 128
CAP = 128
N_BUCKET = 32


def draw_entity_table(key, part):
    key = jax.random.fold_in(key, 11)
    first = jax.random.fold_in(key, 0)
    values = 0.2 * jax.random.normal(first, (ENTITIES, D), jnp.float32)
    return jnp.clip(values, -1.2, 1.2).astype(jnp.bfloat16)


def with_ends(drawn, rng, smallest, top_value):
    place = [jax.random.randint(jax.random.fold_in(rng, axis), (), 0, length) for axis, length in enumerate(drawn.shape)]
    main_axis = drawn.shape.index(max(drawn.shape))
    next_to = place[:main_axis] + [(place[main_axis] + 1) % drawn.shape[main_axis]] + place[main_axis + 1:]
    return drawn.at[tuple(place)].set(smallest).at[tuple(next_to)].set(top_value)


def block_levels(stream_key, extent, cuts, low, top_value):
    def one(axis_at, blocks):
        heights = jax.random.uniform(jax.random.fold_in(jax.random.fold_in(stream_key, 6), axis_at), (blocks,), jnp.float32, low / len(cuts), top_value / len(cuts))
        return jnp.repeat(jnp.exp(heights), extent[axis_at] // blocks).reshape((-1,) + (1,) * (len(extent) - axis_at - 1))

    gain = one(*cuts[0])
    for cut in cuts[1:]:
        gain = gain * one(*cut)
    return gain


def rank_table(amount, slope):
    weights = [(1 << 20) // math.isqrt(standing ** slope) + 1 for standing in range(1, amount + 1)]
    scale = 1 + sum(weights) // (1 << 30)
    return np.cumsum(np.array([max(1, weight // scale) for weight in weights]))


def ranked(stream_key, dims, amount, slope):
    listing = rank_table(amount, slope)
    lot = jax.random.randint(jax.random.fold_in(stream_key, 1), dims, 0, int(listing[amount - 1]))
    standing = jnp.searchsorted(jnp.asarray(listing, jnp.int32), lot, side="right")
    return jax.random.permutation(jax.random.fold_in(stream_key, 2), amount)[standing].astype(jnp.int32)


def shared_out(rng, own, number, rows, amount, top, bound, skew):
    ranking = jax.random.permutation(rng, amount)
    packed, usual = load_shares(amount, rows * top, bound, skew, True), load_shares(amount, rows * top, bound, skew, False)
    places = jnp.arange(amount)

    def named(sizes, turn):
        used = int((sizes > 0).sum())
        fixed = max(1, used // 4)
        moved = fixed + (places - fixed + turn * (used - fixed)) % max(1, amount - fixed)
        return jnp.zeros((amount,), jnp.int32).at[ranking[jnp.where(places < fixed, places, moved)]].set(jnp.asarray(sizes, jnp.int32))

    sizes = jnp.where(number % 4 == 0, named(packed, number // 4), named(usual, number - number // 4 - 1))
    mixed = jax.random.permutation(jax.random.fold_in(own, 3), amount)
    giver, sink = mixed[0:amount // 2 * 2:2], mixed[1:amount // 2 * 2:2]
    margin = jnp.minimum(sizes[giver] - 1, bound - sizes[sink]) // 2
    margin = jnp.where((giver == ranking[0]) | (sink == ranking[0]) | (sizes[sink] == 0), 0, jnp.maximum(margin, 0))
    moved = jax.random.randint(jax.random.fold_in(own, 4), (amount // 2,), 0, 1 << 20) % (margin + 1)
    sizes = sizes.at[giver].add(-moved).at[sink].add(moved)
    items = jnp.searchsorted(jnp.cumsum(sizes), jnp.arange(rows * top), side="right").astype(jnp.int32)
    listing = items.reshape(top, rows).T
    listing = listing[jax.random.permutation(jax.random.fold_in(own, 1), rows)]
    turn = jax.random.randint(jax.random.fold_in(own, 2), (rows, 1), 0, top)
    return jnp.take_along_axis(listing, (jnp.arange(top)[None, :] + turn) % top, axis=1)


def load_shares(number_of, total, reach, skew, full):
    weights = [(1 << 20) // math.isqrt(grade ** skew) + 1 for grade in range(1, number_of + 1)]
    largest = reach if full else min(reach, max(-(-total // number_of), total * weights[0] // sum(weights)))
    least = 1 if total - largest >= number_of - 1 else 0
    counts, spare = [largest] + [least] * (number_of - 1), total - largest - least * (number_of - 1)
    while spare > 0:
        free = [i for i in range(1, number_of) if counts[i] < largest] or [i for i in range(1, number_of) if counts[i] < reach]
        whole, left = sum([weights[i] for i in free]), spare
        for i in free:
            addition = min(reach - counts[i], max(1, left * weights[i] // whole), spare)
            counts[i] = counts[i] + addition
            spare = spare - addition
    return np.array(counts)


def gaussian(rng, shape, width, limit, pieces=(), kind=jnp.bfloat16):
    drawn = jax.random.normal(rng, shape, jnp.float32) * width
    if len(pieces) > 0:
        drawn = block_levels(rng, shape, pieces, -0.22, 0.18) * drawn
    return jnp.clip(drawn, min=-limit, max=limit).astype(kind)


def setup_inputs(seed: int = 0) -> dict:
    streams_of = jax.random.split(jax.random.key(seed), 8)
    entity_table = draw_entity_table(jax.random.fold_in(streams_of[7], 71), 0)
    relation_table = gaussian(streams_of[1], (REL, D), 1.0, 4.0, ((1, 8),))
    head_row = with_ends(jax.random.randint(streams_of[2], (EDGES,), 0, ENT_DEV), jax.random.fold_in(streams_of[2], 1), 0, ENT_DEV - 1).astype(jnp.int32)
    relation_id = with_ends(ranked(streams_of[3], (EDGES,), REL, 2), jax.random.fold_in(streams_of[3], 3), 0, REL - 1).astype(jnp.int32)
    tail_owner_keys = jax.random.split(jax.random.fold_in(streams_of[4], 1), EDGES // EDGES_DEV)
    tail_owner_turns = jax.random.permutation(jax.random.fold_in(streams_of[4], 3), EDGES // EDGES_DEV)
    tail_owner = jax.vmap(lambda own, number: shared_out(jax.random.fold_in(streams_of[4], 2), own, number, EDGES_DEV, N_BUCKET, 1, CAP, 2))(tail_owner_keys, tail_owner_turns).reshape((EDGES, 1))
    tail_row = with_ends(jax.random.randint(streams_of[5], (EDGES,), 0, ENT_DEV), jax.random.fold_in(streams_of[5], 1), 0, ENT_DEV - 1).astype(jnp.int32)
    negative_row = with_ends(jax.random.randint(streams_of[6], (SPANS, NEG), 0, ENT_DEV), jax.random.fold_in(streams_of[6], 1), 0, ENT_DEV - 1).astype(jnp.int32)
    return dict(entity_table=entity_table, relation_table=relation_table, head_row=head_row, relation_id=relation_id, tail_owner=tail_owner, tail_row=tail_row, negative_row=negative_row)


def complex_mul(left, right, sign):
    shape = left.shape
    first = left.reshape(shape[:-1] + (-1, 2, PAIR // 2))
    second = right.reshape(shape[:-1] + (-1, 2, PAIR // 2))
    left_re = first[..., 0, :]
    left_im = first[..., 1, :]
    right_re = second[..., 0, :]
    right_im = sign * second[..., 1, :]
    real_part = left_re * right_re - left_im * right_im
    imag_part = left_re * right_im + left_im * right_re
    return jnp.stack([real_part, imag_part], axis=-2).reshape(shape)


def reference(entity_table, relation_table, head_row, relation_id, tail_owner, tail_row, negative_row):
    group = jnp.arange(EDGES, dtype=jnp.int32) // EDGES_DEV
    heads = (group * ENT_DEV + head_row).astype(jnp.int32)
    tails = (tail_owner[:, 0] * ENT_DEV + tail_row).astype(jnp.int32)
    span_group = (jnp.arange(SPANS, dtype=jnp.int32) * SPAN) // EDGES_DEV
    negatives = (span_group[:, None] * ENT_DEV + negative_row).astype(jnp.int32)
    head_emb = entity_table[heads].astype(jnp.float32)
    rel_emb = relation_table[relation_id].astype(jnp.float32)
    product = complex_mul(head_emb, rel_emb, 1.0).astype(jnp.bfloat16)
    tail_emb = entity_table[tails]
    positive = jnp.sum(product.astype(jnp.float32) * tail_emb.astype(jnp.float32), axis=1)

    def span_step(grad, inputs):
        prod, pos, negs = inputs
        neg_emb = entity_table[negs]
        scores = jnp.dot(prod, neg_emb.T, preferred_element_type=jnp.float32)
        top = jnp.maximum(jnp.max(scores, axis=1), pos)
        expo = jnp.exp(scores - top[:, None])
        expo_pos = jnp.exp(pos - top)
        total = jnp.sum(expo, axis=1) + expo_pos
        loss = top + jnp.log(total) - pos
        weight = (expo / total[:, None]).astype(jnp.bfloat16)
        pos_grad = expo_pos / total - 1.0
        prod_grad = jnp.dot(weight, neg_emb, preferred_element_type=jnp.float32)
        neg_grad = jnp.dot(weight.T, prod, preferred_element_type=jnp.float32)
        grad = grad.at[negs].add(neg_grad)
        return grad, (loss, prod_grad, pos_grad)

    start = jnp.zeros((ENTITIES, D), jnp.float32)
    inputs = (product.reshape(SPANS, SPAN, D), positive.reshape(SPANS, SPAN), negatives)
    grad, (loss, prod_grad, pos_grad) = lax.scan(span_step, start, inputs)
    loss = loss.reshape(EDGES)
    pos_grad = pos_grad.reshape(EDGES)
    prod_grad = prod_grad.reshape(EDGES, D) + pos_grad[:, None] * tail_emb.astype(jnp.float32)
    head_grad = complex_mul(prod_grad, rel_emb, -1.0)
    rel_grad = complex_mul(prod_grad, head_emb, -1.0)
    grad = grad.at[heads].add(head_grad)
    grad = grad.at[tails].add(pos_grad[:, None] * product.astype(jnp.float32))
    relation_grad = jnp.zeros((REL, D), jnp.float32).at[relation_id].add(rel_grad)
    return loss, grad, relation_grad
```

```python
import functools

import jax
import jax.numpy as jnp
from jax import lax
from jax.experimental import pallas as pl
from jax.experimental.pallas import tpu as pltpu
from jax.sharding import PartitionSpec as P

LANES = 128
SPAN = 512
NEG_PAD = 1024
ROWS = 8192
DUMP = 8192
RELS = 4096
EDGES = 2048
BUCKETS = 32
CHIPS = 4
F32 = jnp.float32
BF16 = jnp.bfloat16
VM = pl.BlockSpec(memory_space=pltpu.VMEM)
SM = pl.BlockSpec(memory_space=pltpu.SMEM)
NT = (((1,), (1,)), ((), ()))
TN = (((0,), (0,)), ((), ()))


def call(kernel, name, outs, ins, scratch=(), flops=1000000, size=4000000):
    return pl.pallas_call(
        kernel,
        name=name,
        out_shape=outs,
        in_specs=ins,
        out_specs=jax.tree.map(lambda _: VM, outs),
        scratch_shapes=scratch,
        compiler_params=pltpu.CompilerParams(vmem_limit_bytes=56 << 20),
        cost_estimate=pl.CostEstimate(flops=flops, bytes_accessed=size, transcendentals=0),
    )


def shape(dims, kind):
    return jax.ShapeDtypeStruct(dims, kind)


def iota(dims, axis):
    return lax.broadcasted_iota(jnp.int32, dims, axis)


def to_column(row):
    size = row.shape[1]
    same = iota((size, size), 0) == iota((size, size), 1)
    return jnp.sum(jnp.where(same, row, 0.0), axis=1, keepdims=True)


def to_row(column):
    size = column.shape[0]
    same = iota((size, size), 0) == iota((size, size), 1)
    return jnp.sum(jnp.where(same, column, 0.0), axis=0, keepdims=True)


def swap_halves(value):
    return pltpu.roll(value, LANES // 2, 1)


def times(left, right):
    lane = iota(left.shape, 1)
    first = lane < LANES // 2
    turned = swap_halves(right)
    real = jnp.where(first, right, turned)
    imag = jnp.where(first, -turned, right)
    return left * real + swap_halves(left) * imag


def times_conj(left, right):
    lane = iota(left.shape, 1)
    first = lane < LANES // 2
    turned = swap_halves(right)
    real = jnp.where(first, right, turned)
    imag = jnp.where(first, turned, -right)
    return left * real + swap_halves(left) * imag


def rank_kernel(owner_ref, row_ref, target_ref, request_ref):
    lower = (iota((LANES, LANES), 0) <= iota((LANES, LANES), 1)).astype(BF16)
    before = jnp.zeros((BUCKETS, 1), F32)
    high = jnp.zeros((BUCKETS, LANES), F32)
    low = jnp.zeros((BUCKETS, LANES), F32)
    for block in range(EDGES // LANES):
        at = slice(block * LANES, (block + 1) * LANES)
        owner = owner_ref[:, at]
        row = row_ref[:, at]
        mine = iota((BUCKETS, LANES), 0) == owner
        hit = mine.astype(F32).astype(BF16)
        count = jnp.dot(hit, lower, preferred_element_type=F32)
        place = jnp.where(mine, count + before - 1.0, 0.0)
        rank = jnp.sum(place, axis=0, keepdims=True)
        before = before + count[:, LANES - 1 : LANES]
        target_ref[:, at] = owner * LANES + rank.astype(jnp.int32)
        slot = iota((LANES, LANES), 0) == rank.astype(jnp.int32)
        upper = jnp.where(slot, (row >> 7).astype(F32), 0.0).astype(BF16)
        under = jnp.where(slot, (row & 127).astype(F32), 0.0).astype(BF16)
        high = high + lax.dot_general(hit, upper, NT, preferred_element_type=F32)
        low = low + lax.dot_general(hit, under, NT, preferred_element_type=F32)
    used = iota((BUCKETS, LANES), 1).astype(F32) < before
    request_ref[...] = jnp.where(used, high * 128.0 + low, float(DUMP)).astype(jnp.int32)


def load_table(table_ref, wide_ref, rows):
    wide_ref[0:rows, :] = table_ref[...].astype(F32)


def gather_kernel(unroll, chip_ref, head_ref, rel_ref, neg_ref, table_ref, rtable_ref,
                  p0, p1, p2, p3, product_ref, heads_ref, rels_ref, negs_ref, wide, rwide):
    load_table(table_ref, wide, ROWS)
    load_table(rtable_ref, rwide, RELS)
    wide[ROWS : ROWS + 8, :] = jnp.zeros((8, LANES), F32)
    for step, pack in enumerate((p0, p1, p2, p3)):
        span = lax.rem(chip_ref[0] + step, CHIPS)

        def edge_step(j, carry):
            base = pl.multiple_of(span * SPAN + j * unroll, unroll)
            head = jnp.concatenate(
                [wide[pl.ds(head_ref[base + r], 1), :] for r in range(unroll)], axis=0)
            rel = jnp.concatenate(
                [rwide[pl.ds(rel_ref[base + r], 1), :] for r in range(unroll)], axis=0)
            product = times(head, rel).astype(BF16)
            at = pl.ds(base, unroll)
            pack[pl.ds(pl.multiple_of(NEG_PAD + j * unroll, unroll), unroll), :] = product
            product_ref[at, :] = product
            heads_ref[at, :] = head.astype(BF16)
            rels_ref[at, :] = rel.astype(BF16)
            return carry

        lax.fori_loop(0, SPAN // unroll, edge_step, 0)

        def neg_step(j, carry):
            base = pl.multiple_of(j * unroll, unroll)
            rows = jnp.concatenate(
                [wide[pl.ds(neg_ref[span, base + r], 1), :] for r in range(unroll)],
                axis=0).astype(BF16)
            pack[pl.ds(base, unroll), :] = rows
            negs_ref[span, pl.ds(base, unroll), :] = rows
            return carry

        lax.fori_loop(0, NEG_PAD // unroll, neg_step, 0)


def found_kernel(unroll, asked_ref, table_ref, found_ref, wide):
    load_table(table_ref, wide, ROWS)
    wide[ROWS : ROWS + 8, :] = jnp.zeros((8, LANES), F32)

    def source(s, carry):
        def group(j):
            base = pl.multiple_of(j * unroll, unroll)
            rows = jnp.concatenate(
                [wide[pl.ds(asked_ref[s, base + r], 1), :] for r in range(unroll)], axis=0)
            found_ref[s, pl.ds(base, unroll), :] = rows.astype(BF16)
            return j + 1

        def more(j):
            first = asked_ref[s, jnp.minimum(j * unroll, LANES - 1)]
            return jnp.logical_and(j * unroll < LANES, first < DUMP)

        lax.while_loop(more, group, 0)
        return carry

    lax.fori_loop(0, BUCKETS, source, 0)


def tail_kernel(unroll, target_ref, fetched_ref, product_ref, tails_ref, partial_ref, slots_ref,
                wide, out_wide, prod_wide):
    wide[...] = fetched_ref[...].astype(F32)
    prod_wide[...] = product_ref[...].astype(F32)
    out_wide[...] = jnp.zeros_like(out_wide)

    def step(j, carry):
        base = pl.multiple_of(j * unroll, unroll)
        rows = []
        for r in range(unroll):
            place = target_ref[0, base + r]
            rows.append(wide[pl.ds(place, 1), :])
            out_wide[pl.ds(place, 1), :] = prod_wide[pl.ds(base + r, 1), :]
        tails_ref[pl.ds(base, unroll), :] = jnp.concatenate(rows, axis=0).astype(BF16)
        return carry

    lax.fori_loop(0, EDGES // unroll, step, 0)
    slots_ref[...] = out_wide[...].astype(BF16)
    for block in range(EDGES // LANES):
        at = slice(block * LANES, (block + 1) * LANES)
        both = tails_ref[at, :].astype(F32) * prod_wide[at, :]
        partial_ref[:, at] = to_row(jnp.sum(both, axis=1, keepdims=True))


def score_kernel(core_ref, q0, q1, q2, q3, keep_ref, send_ref):
    core = core_ref[0]
    parts = (q0, q1, q2, q3)
    for half, out in ((core, keep_ref), (1 - core, send_ref)):
        at = pl.ds(pl.multiple_of(NEG_PAD + half * (SPAN // 2), SPAN // 2), SPAN // 2)
        left = jnp.concatenate([q[at, :] for q in parts], axis=1)
        for piece in range(4):
            cut = slice(piece * 256, (piece + 1) * 256)
            right = jnp.concatenate([q[cut, :] for q in parts], axis=1)
            out[:, cut] = lax.dot_general(left, right, NT, preferred_element_type=F32)


def soft_kernel(negatives, keep_ref, other_ref, weight_ref, stat_ref):
    for block in range(SPAN // 2 // LANES):
        at = slice(block * LANES, (block + 1) * LANES)
        scores = keep_ref[at, :] + other_ref[at, :]
        real = iota((LANES, NEG_PAD), 1) < negatives
        scores = jnp.where(real, scores, -jnp.inf)
        top = jnp.max(scores, axis=1, keepdims=True)
        expo = jnp.exp(scores - top)
        weight_ref[at, :] = expo.astype(BF16)
        stat_ref[0:1, at] = to_row(top)
        stat_ref[1:2, at] = to_row(jnp.sum(expo, axis=1, keepdims=True))


def edge_kernel(unroll, rel_ref, target_ref, positive_ref, stat_ref, weight_ref, negs_ref,
                product_ref, heads_ref, rels_ref, tails_ref,
                loss_ref, head_grad_ref, rel_grad_ref, slot_ref, scaled_ref,
                grad, a0, a1, a2, a3):
    sums = (a0, a1, a2, a3)
    for one in sums:
        one[...] = jnp.zeros_like(one)
    slots = jnp.zeros((BUCKETS, LANES), F32)
    half = SPAN // 2
    for block in range(EDGES // LANES):
        at = slice(block * LANES, (block + 1) * LANES)
        part, inner = block // 2, (block % 2) * LANES
        high = stat_ref[part, 0:1, inner : inner + LANES]
        mass = stat_ref[part, 1:2, inner : inner + LANES]
        positive = positive_ref[:, at]
        top = jnp.maximum(high, positive)
        shrink = jnp.exp(high - top)
        expo = jnp.exp(positive - top)
        total = mass * shrink + expo
        scale = shrink / total
        slope = expo / total - 1.0
        loss_ref[:, at] = top + jnp.log(total) - positive
        target = target_ref[:, at]
        hit = (iota((BUCKETS, LANES), 0) == (target >> 7)).astype(F32).astype(BF16)
        slot = iota((LANES, LANES), 0) == (target & 127)
        rest = slope
        for _ in range(3):
            piece = rest.astype(BF16)
            spread = jnp.where(slot, piece.astype(F32), 0.0).astype(BF16)
            slots = slots + lax.dot_general(hit, spread, NT, preferred_element_type=F32)
            rest = rest - piece.astype(F32)
        scale_col = to_column(scale)
        slope_col = to_column(slope)
        scaled_ref[at, :] = (product_ref[at, :].astype(F32) * scale_col).astype(BF16)
        raw = jnp.dot(weight_ref[at, :], negs_ref[block // 4], preferred_element_type=F32)
        down = raw * scale_col + slope_col * tails_ref[at, :].astype(F32)
        head_grad_ref[at, :] = times_conj(down, rels_ref[at, :].astype(F32))
        grad[at, :] = times_conj(down, heads_ref[at, :].astype(F32))
    slot_ref[...] = slots

    def step(j, carry):
        for r in range(unroll):
            for k, one in enumerate(sums):
                edge = k * SPAN + j * unroll + r
                place = pl.ds(rel_ref[edge], 1)
                one[place, :] = one[place, :] + grad[pl.ds(edge, 1), :]
        return carry

    lax.fori_loop(0, SPAN // unroll, step, 0)
    rel_grad_ref[...] = ((a0[...] + a1[...]) + (a2[...] + a3[...])).astype(BF16)


def entity_kernel(unroll, negatives, head_ref, neg_ref, weight_ref, scaled_ref, head_grad_ref,
                  out_ref, grad, a0, a1, a2, a3):
    sums = (a0, a1, a2, a3)
    for one in sums:
        one[...] = jnp.zeros_like(one)
    for span in range(CHIPS):
        at = slice(span * SPAN, (span + 1) * SPAN)
        grad[span] = lax.dot_general(
            weight_ref[at, :], scaled_ref[at, :], TN, preferred_element_type=F32)

    def edge_step(j, carry):
        for r in range(unroll):
            for k, one in enumerate(sums):
                edge = k * SPAN + j * unroll + r
                place = pl.ds(head_ref[edge], 1)
                one[place, :] = one[place, :] + head_grad_ref[pl.ds(edge, 1), :]
        return carry

    lax.fori_loop(0, SPAN // unroll, edge_step, 0)

    def neg_step(j, carry):
        for r in range(unroll):
            for k, one in enumerate(sums):
                place = pl.ds(neg_ref[k, j * unroll + r], 1)
                one[place, :] = one[place, :] + grad[k, pl.ds(j * unroll + r, 1), :]
        return carry

    lax.fori_loop(0, negatives // unroll, neg_step, 0)
    total = (a0[0:ROWS, :] + a1[0:ROWS, :]) + (a2[0:ROWS, :] + a3[0:ROWS, :])
    out_ref[...] = total


def owner_kernel(unroll, asked_ref, slope_ref, came_ref, part_ref, out_ref,
                 wide, a0, a1, a2, a3):
    sums = (a0, a1, a2, a3)
    for one in sums[1:]:
        one[...] = jnp.zeros_like(one)
    a0[0:ROWS, :] = part_ref[...]
    a0[ROWS : ROWS + 8, :] = jnp.zeros((8, LANES), F32)
    wide[...] = came_ref[...].astype(F32)
    each = BUCKETS // 4

    def source(s, carry):
        def group(j):
            for r in range(unroll):
                for k, one in enumerate(sums):
                    owner = k * each + s
                    slot = j * unroll + r
                    place = pl.ds(asked_ref[owner, slot], 1)
                    term = slope_ref[owner, slot] * wide[pl.ds(owner * LANES + slot, 1), :]
                    one[place, :] = one[place, :] + term
            return j + 1

        def more(j):
            at = jnp.minimum(j * unroll, LANES - 1)
            first = asked_ref[s, at]
            for k in range(1, 4):
                first = jnp.minimum(first, asked_ref[k * each + s, at])
            return jnp.logical_and(j * unroll < LANES, first < DUMP)

        lax.while_loop(more, group, 0)
        return carry

    lax.fori_loop(0, each, source, 0)
    total = (a0[0:ROWS, :] + a1[0:ROWS, :]) + (a2[0:ROWS, :] + a3[0:ROWS, :])
    out_ref[...] = total


def body(entity_table, relation_table, head_row, relation_id, tail_owner, tail_row, negative_row):
    negatives = negative_row.shape[1]
    place = lax.axis_index("col")
    chip = (place // 2).astype(jnp.int32).reshape(1)
    core = (place % 2).astype(jnp.int32).reshape(1)
    pad = jnp.pad(negative_row, ((0, 0), (0, NEG_PAD - negatives)), constant_values=DUMP)
    pack = shape((NEG_PAD + SPAN, LANES), BF16)
    flat = shape((EDGES, LANES), BF16)
    wide = pltpu.VMEM((ROWS + 8, LANES), F32)

    target, request = call(
        rank_kernel, "rank",
        (shape((1, EDGES), jnp.int32), shape((BUCKETS, LANES), jnp.int32)), [VM, VM],
    )(tail_owner.reshape(1, EDGES), tail_row.reshape(1, EDGES))
    asked = lax.all_to_all(request, "bucket", split_axis=0, concat_axis=0, tiled=True)

    p0, p1, p2, p3, product, heads, rels, negs = call(
        functools.partial(gather_kernel, 32), "gather",
        (pack, pack, pack, pack, flat, flat, flat, shape((CHIPS, NEG_PAD, LANES), BF16)),
        [SM, SM, SM, SM, VM, VM],
        [wide, pltpu.VMEM((RELS, LANES), F32)], size=30000000,
    )(chip, head_row, relation_id, pad, entity_table, relation_table)

    def along(step):
        return [(2 * x + c, 2 * ((x + step) % CHIPS) + c) for x in range(CHIPS) for c in range(2)]

    q1 = lax.ppermute(p1, "col", along(1))
    q2 = lax.ppermute(p2, "col", along(2))
    q3 = lax.ppermute(p3, "col", along(3))

    found = call(
        functools.partial(found_kernel, 32), "found",
        shape((BUCKETS, LANES, LANES), BF16), [SM, VM], [wide], size=15000000,
    )(asked, entity_table)
    fetched = lax.all_to_all(found, "bucket", split_axis=0, concat_axis=0, tiled=True)

    half = shape((SPAN // 2, NEG_PAD), F32)
    keep, send = call(score_kernel, "scores", (half, half), [SM, VM, VM, VM, VM],
                      flops=500000000)(core, p0, q1, q2, q3)
    other = lax.ppermute(send, "col", [(c, c ^ 1) for c in range(8)])
    weight, stat = call(
        functools.partial(soft_kernel, negatives), "soft",
        (shape((SPAN // 2, NEG_PAD), BF16), shape((2, SPAN // 2), F32)), [VM, VM],
    )(keep, other)
    weights = lax.all_gather(weight, "col", axis=0, tiled=True)
    stats = lax.all_gather(stat, "col", axis=0)

    tails, partial, slots = call(
        functools.partial(tail_kernel, 32), "tails",
        (flat, shape((1, EDGES), F32), shape((BUCKETS * LANES, LANES), BF16)), [SM, VM, VM],
        [pltpu.VMEM((BUCKETS * LANES, LANES), F32), pltpu.VMEM((BUCKETS * LANES, LANES), F32),
         pltpu.VMEM((EDGES, LANES), F32)], size=15000000,
    )(target, fetched.reshape(BUCKETS * LANES, LANES), product)
    positive = lax.psum(partial, "col")
    came = lax.all_to_all(slots.reshape(BUCKETS, LANES, LANES), "bucket",
                          split_axis=0, concat_axis=0, tiled=True)

    loss, head_grad, rel_local, slope, scaled = call(
        functools.partial(edge_kernel, 8), "edges",
        (shape((1, EDGES), F32), shape((EDGES, LANES), F32), shape((RELS, LANES), BF16),
         shape((BUCKETS, LANES), F32), flat),
        [SM] + [VM] * 9,
        [pltpu.VMEM((EDGES, LANES), F32)] + [pltpu.VMEM((RELS, LANES), F32)] * 4,
        size=20000000,
    )(relation_id, target, positive, stats, weights, negs, product, heads, rels, tails)
    slopes = lax.all_to_all(slope, "bucket", split_axis=0, concat_axis=0, tiled=True)
    rel_parts = lax.all_to_all(rel_local.reshape(BUCKETS, LANES, LANES), "bucket",
                               split_axis=0, concat_axis=0, tiled=True)

    part = call(
        functools.partial(entity_kernel, 8, negatives), "entities", shape((ROWS, LANES), F32),
        [SM, SM, VM, VM, VM],
        [pltpu.VMEM((CHIPS, NEG_PAD, LANES), F32)] + [wide] * 4, size=40000000,
    )(head_row, pad, weights, scaled, head_grad)
    grad = call(
        functools.partial(owner_kernel, 8), "owners", shape((ROWS, LANES), F32),
        [SM, SM, VM, VM],
        [pltpu.VMEM((BUCKETS * LANES, LANES), F32)] + [wide] * 4, size=30000000,
    )(asked, slopes, came.reshape(BUCKETS * LANES, LANES), part)
    relation_grad = jnp.sum(rel_parts.astype(F32), axis=0)
    return (loss.reshape(EDGES), grad, relation_grad)


def solution(mesh):
    in_specs = (
        P("bucket", "col"),
        P(None, "col"),
        P("bucket"),
        P("bucket"),
        P("bucket", None),
        P("bucket"),
        P("bucket", None),
    )
    out_specs = (P("bucket"), P("bucket", "col"), P("bucket", "col"))
    return jax.shard_map(body, mesh=mesh, in_specs=in_specs, out_specs=out_specs, check_vma=False)
```

```python
import functools

import jax
import jax.numpy as jnp
from jax import lax
from jax.experimental import pallas as pl
from jax.experimental.pallas import tpu as pltpu
from jax.sharding import PartitionSpec as P

LANES = 128
SPAN = 512
NEG_PAD = 1024
ROWS = 8192
DUMP = 8192
RELS = 4096
EDGES = 2048
BUCKETS = 32
CHIPS = 4
F32 = jnp.float32
BF16 = jnp.bfloat16
VM = pl.BlockSpec(memory_space=pltpu.VMEM)
SM = pl.BlockSpec(memory_space=pltpu.SMEM)
NT = (((1,), (1,)), ((), ()))
TN = (((0,), (0,)), ((), ()))


def call(kernel, name, outs, ins, scratch=(), flops=1000000, size=4000000, group=None):
    remote = {} if group is None else dict(collective_id=group, has_side_effects=True)
    return pl.pallas_call(
        kernel,
        name=name,
        out_shape=outs,
        in_specs=ins,
        out_specs=jax.tree.map(lambda _: VM, outs),
        scratch_shapes=scratch,
        compiler_params=pltpu.CompilerParams(vmem_limit_bytes=56 << 20, **remote),
        cost_estimate=pl.CostEstimate(flops=flops, bytes_accessed=size, transcendentals=0),
    )


def shape(dims, kind):
    return jax.ShapeDtypeStruct(dims, kind)


def iota(dims, axis):
    return lax.broadcasted_iota(jnp.int32, dims, axis)


def to_column(row):
    size = row.shape[1]
    same = iota((size, size), 0) == iota((size, size), 1)
    return jnp.sum(jnp.where(same, row, 0.0), axis=1, keepdims=True)


def to_row(column):
    size = column.shape[0]
    same = iota((size, size), 0) == iota((size, size), 1)
    return jnp.sum(jnp.where(same, column, 0.0), axis=0, keepdims=True)


def swap_halves(value):
    return pltpu.roll(value, LANES // 2, 1)


def times(left, right):
    lane = iota(left.shape, 1)
    first = lane < LANES // 2
    turned = swap_halves(right)
    real = jnp.where(first, right, turned)
    imag = jnp.where(first, -turned, right)
    return left * real + swap_halves(left) * imag


def times_conj(left, right):
    lane = iota(left.shape, 1)
    first = lane < LANES // 2
    turned = swap_halves(right)
    real = jnp.where(first, right, turned)
    imag = jnp.where(first, turned, -right)
    return left * real + swap_halves(left) * imag


def greet(axis, count):
    me = lax.axis_index(axis)
    barrier = pltpu.get_barrier_semaphore()

    def tell(i, carry):
        peer = lax.rem(me + i, count)
        pl.semaphore_signal(barrier, inc=1, device_id={axis: peer},
                            device_id_type=pl.DeviceIdType.MESH)
        return carry

    lax.fori_loop(1, count, tell, 0)
    pl.semaphore_wait(barrier, count - 1)


def spread(axis, count, src, dst, send_sem, recv_sem):
    me = lax.axis_index(axis)

    def send(i, carry):
        peer = lax.rem(me + i, count)
        pltpu.make_async_remote_copy(
            src_ref=src.at[peer], dst_ref=dst.at[me], send_sem=send_sem, recv_sem=recv_sem,
            device_id={axis: peer}, device_id_type=pl.DeviceIdType.MESH).start()
        return carry

    lax.fori_loop(1, count, send, 0)


def settle(axis, count, src, dst, send_sem, recv_sem):
    me = lax.axis_index(axis)
    rest = pl.ds(0, count - 1)
    pltpu.make_async_remote_copy(
        src_ref=src.at[rest], dst_ref=dst.at[rest], send_sem=send_sem, recv_sem=recv_sem,
        device_id={axis: lax.rem(me + 1, count)}, device_id_type=pl.DeviceIdType.MESH).wait()


def slope_kernel(slope_ref, out_ref, send_sem, recv_sem):
    greet("bucket", BUCKETS)
    spread("bucket", BUCKETS, slope_ref, out_ref, send_sem, recv_sem)
    me = lax.axis_index("bucket")
    out_ref[me] = slope_ref[me]
    settle("bucket", BUCKETS, slope_ref, out_ref, send_sem, recv_sem)


def share_kernel(cols, partial_ref, stat_ref, positive_ref, stats_ref, parts,
                 send_sem, recv_sem):
    greet("col", cols)
    me = lax.axis_index("col")
    kept = (partial_ref, stat_ref)
    lands = (parts, stats_ref)

    def send(i, carry):
        peer = lax.rem(me + i, cols)
        for k in range(2):
            pltpu.make_async_remote_copy(
                src_ref=kept[k], dst_ref=lands[k].at[me], send_sem=send_sem.at[k],
                recv_sem=recv_sem.at[k], device_id={"col": peer},
                device_id_type=pl.DeviceIdType.MESH).start()
        return carry

    lax.fori_loop(1, cols, send, 0)
    parts[me] = partial_ref[...]
    stats_ref[me] = stat_ref[...]
    rest = pl.ds(0, cols - 1)
    for k in range(2):
        pltpu.make_async_remote_copy(
            src_ref=lands[k].at[rest], dst_ref=lands[k].at[rest], send_sem=send_sem.at[k],
            recv_sem=recv_sem.at[k], device_id={"col": lax.rem(me + 1, cols)},
            device_id_type=pl.DeviceIdType.MESH).wait()
    total = parts[0]
    for k in range(1, cols):
        total = total + parts[k]
    positive_ref[...] = total


def rank_kernel(owner_ref, row_ref, target_ref, asked_ref, request_ref, send_sem, recv_sem):
    lower = (iota((LANES, LANES), 0) <= iota((LANES, LANES), 1)).astype(BF16)
    before = jnp.zeros((BUCKETS, 1), F32)
    high = jnp.zeros((BUCKETS, LANES), F32)
    low = jnp.zeros((BUCKETS, LANES), F32)
    for block in range(EDGES // LANES):
        at = slice(block * LANES, (block + 1) * LANES)
        owner = owner_ref[:, at]
        row = row_ref[:, at]
        mine = iota((BUCKETS, LANES), 0) == owner
        hit = mine.astype(F32).astype(BF16)
        count = jnp.dot(hit, lower, preferred_element_type=F32)
        place = jnp.where(mine, count + before - 1.0, 0.0)
        rank = jnp.sum(place, axis=0, keepdims=True)
        before = before + count[:, LANES - 1 : LANES]
        target_ref[:, at] = owner * LANES + rank.astype(jnp.int32)
        slot = iota((LANES, LANES), 0) == rank.astype(jnp.int32)
        upper = jnp.where(slot, (row >> 7).astype(F32), 0.0).astype(BF16)
        under = jnp.where(slot, (row & 127).astype(F32), 0.0).astype(BF16)
        high = high + lax.dot_general(hit, upper, NT, preferred_element_type=F32)
        low = low + lax.dot_general(hit, under, NT, preferred_element_type=F32)
    used = iota((BUCKETS, LANES), 1).astype(F32) < before
    request = jnp.where(used, high * 128.0 + low, float(DUMP)).astype(jnp.int32)
    for owner in range(BUCKETS):
        request_ref[owner] = request[owner : owner + 1, :]
    greet("bucket", BUCKETS)
    spread("bucket", BUCKETS, request_ref, asked_ref, send_sem, recv_sem)
    me = lax.axis_index("bucket")
    asked_ref[me] = request_ref[me]
    settle("bucket", BUCKETS, request_ref, asked_ref, send_sem, recv_sem)


def load_table(table_ref, wide_ref, rows):
    wide_ref[0:rows, :] = table_ref[...].astype(F32)


def gather_kernel(unroll, chip_ref, head_ref, rel_ref, neg_ref, table_ref, rtable_ref,
                  p0, p1, p2, p3, product_ref, heads_ref, rels_ref, negs_ref, wide, rwide):
    load_table(table_ref, wide, ROWS)
    load_table(rtable_ref, rwide, RELS)
    wide[ROWS : ROWS + 8, :] = jnp.zeros((8, LANES), F32)
    for step, pack in enumerate((p0, p1, p2, p3)):
        span = lax.rem(chip_ref[0] + step, CHIPS)

        def edge_step(j, carry):
            base = pl.multiple_of(span * SPAN + j * unroll, unroll)
            head = jnp.concatenate(
                [wide[pl.ds(head_ref[base + r], 1), :] for r in range(unroll)], axis=0)
            rel = jnp.concatenate(
                [rwide[pl.ds(rel_ref[base + r], 1), :] for r in range(unroll)], axis=0)
            product = times(head, rel).astype(BF16)
            at = pl.ds(base, unroll)
            pack[pl.ds(pl.multiple_of(NEG_PAD + j * unroll, unroll), unroll), :] = product
            product_ref[at, :] = product
            heads_ref[at, :] = head.astype(BF16)
            rels_ref[at, :] = rel.astype(BF16)
            return carry

        lax.fori_loop(0, SPAN // unroll, edge_step, 0)

        def neg_step(j, carry):
            base = pl.multiple_of(j * unroll, unroll)
            rows = jnp.concatenate(
                [wide[pl.ds(neg_ref[span * NEG_PAD + j * unroll + r], 1), :] for r in range(unroll)],
                axis=0).astype(BF16)
            pack[pl.ds(base, unroll), :] = rows
            negs_ref[span, pl.ds(base, unroll), :] = rows
            return carry

        lax.fori_loop(0, NEG_PAD // unroll, neg_step, 0)


def found_kernel(unroll, asked_ref, table_ref, found_ref, wide):
    load_table(table_ref, wide, ROWS)
    wide[ROWS : ROWS + 8, :] = jnp.zeros((8, LANES), F32)

    def source(s, carry):
        def group(j):
            base = pl.multiple_of(j * unroll, unroll)
            rows = jnp.concatenate(
                [wide[pl.ds(asked_ref[s * LANES + j * unroll + r], 1), :] for r in range(unroll)], axis=0)
            found_ref[s, pl.ds(base, unroll), :] = rows.astype(BF16)
            return j + 1

        def more(j):
            first = asked_ref[s * LANES + jnp.minimum(j * unroll, LANES - 1)]
            return jnp.logical_and(j * unroll < LANES, first < DUMP)

        lax.while_loop(more, group, 0)
        return carry

    lax.fori_loop(0, BUCKETS, source, 0)


def tail_kernel(unroll, target_ref, fetched_ref, product_ref, tails_ref, partial_ref, slots_ref,
                wide, out_wide, prod_wide):
    wide[...] = fetched_ref[...].astype(F32)
    prod_wide[...] = product_ref[...].astype(F32)
    out_wide[...] = jnp.zeros_like(out_wide)

    def step(j, carry):
        base = pl.multiple_of(j * unroll, unroll)
        rows = []
        for r in range(unroll):
            place = target_ref[base + r]
            rows.append(wide[pl.ds(place, 1), :])
            out_wide[pl.ds(place, 1), :] = prod_wide[pl.ds(base + r, 1), :]
        tails_ref[pl.ds(base, unroll), :] = jnp.concatenate(rows, axis=0).astype(BF16)
        return carry

    lax.fori_loop(0, EDGES // unroll, step, 0)
    slots_ref[...] = out_wide[...].astype(BF16)
    for block in range(EDGES // LANES):
        at = slice(block * LANES, (block + 1) * LANES)
        both = tails_ref[at, :].astype(F32) * prod_wide[at, :]
        partial_ref[:, at] = to_row(jnp.sum(both, axis=1, keepdims=True))


def score_kernel(core_ref, q0, q1, q2, q3, keep_ref, send_ref):
    core = core_ref[0]
    parts = (q0, q1, q2, q3)
    for half, out in ((core, keep_ref), (1 - core, send_ref)):
        at = pl.ds(pl.multiple_of(NEG_PAD + half * (SPAN // 2), SPAN // 2), SPAN // 2)
        left = jnp.concatenate([q[at, :] for q in parts], axis=1)
        for piece in range(4):
            cut = slice(piece * 256, (piece + 1) * 256)
            right = jnp.concatenate([q[cut, :] for q in parts], axis=1)
            out[:, cut] = lax.dot_general(left, right, NT, preferred_element_type=F32)


def soft_kernel(negatives, keep_ref, other_ref, weight_ref, stat_ref):
    for block in range(SPAN // 2 // LANES):
        at = slice(block * LANES, (block + 1) * LANES)
        scores = keep_ref[at, :] + other_ref[at, :]
        real = iota((LANES, NEG_PAD), 1) < negatives
        scores = jnp.where(real, scores, -jnp.inf)
        top = jnp.max(scores, axis=1, keepdims=True)
        expo = jnp.exp(scores - top)
        weight_ref[at, :] = expo.astype(BF16)
        stat_ref[0:1, at] = to_row(top)
        stat_ref[1:2, at] = to_row(jnp.sum(expo, axis=1, keepdims=True))


def edge_kernel(unroll, rel_ref, target_ref, positive_ref, stat_ref, weight_ref, negs_ref,
                product_ref, heads_ref, rels_ref, tails_ref,
                loss_ref, head_grad_ref, rel_grad_ref, slot_ref, scaled_ref,
                grad, a0, a1, a2, a3):
    sums = (a0, a1, a2, a3)
    for one in sums:
        one[...] = jnp.zeros_like(one)
    slots = jnp.zeros((BUCKETS, LANES), F32)
    half = SPAN // 2
    for block in range(EDGES // LANES):
        at = slice(block * LANES, (block + 1) * LANES)
        part, inner = block // 2, (block % 2) * LANES
        high = stat_ref[part, 0:1, inner : inner + LANES]
        mass = stat_ref[part, 1:2, inner : inner + LANES]
        positive = positive_ref[:, at]
        top = jnp.maximum(high, positive)
        shrink = jnp.exp(high - top)
        expo = jnp.exp(positive - top)
        total = mass * shrink + expo
        scale = shrink / total
        slope = expo / total - 1.0
        loss_ref[:, at] = top + jnp.log(total) - positive
        target = target_ref[:, at]
        hit = (iota((BUCKETS, LANES), 0) == (target >> 7)).astype(F32).astype(BF16)
        slot = iota((LANES, LANES), 0) == (target & 127)
        rest = slope
        for _ in range(3):
            piece = rest.astype(BF16)
            spread = jnp.where(slot, piece.astype(F32), 0.0).astype(BF16)
            slots = slots + lax.dot_general(hit, spread, NT, preferred_element_type=F32)
            rest = rest - piece.astype(F32)
        scale_col = to_column(scale)
        slope_col = to_column(slope)
        scaled_ref[at, :] = (product_ref[at, :].astype(F32) * scale_col).astype(BF16)
        raw = jnp.dot(weight_ref[at, :], negs_ref[block // 4], preferred_element_type=F32)
        down = raw * scale_col + slope_col * tails_ref[at, :].astype(F32)
        head_grad_ref[at, :] = times_conj(down, rels_ref[at, :].astype(F32))
        grad[at, :] = times_conj(down, heads_ref[at, :].astype(F32))
    for owner in range(BUCKETS):
        slot_ref[owner] = slots[owner : owner + 1, :]

    def step(j, carry):
        for r in range(unroll):
            for k, one in enumerate(sums):
                edge = k * SPAN + j * unroll + r
                place = pl.ds(rel_ref[edge], 1)
                one[place, :] = one[place, :] + grad[pl.ds(edge, 1), :]
        return carry

    lax.fori_loop(0, SPAN // unroll, step, 0)
    rel_grad_ref[...] = ((a0[...] + a1[...]) + (a2[...] + a3[...])).astype(BF16)


def entity_kernel(unroll, negatives, head_ref, neg_ref, weight_ref, scaled_ref, head_grad_ref,
                  out_ref, grad, a0, a1, a2, a3):
    sums = (a0, a1, a2, a3)
    for one in sums:
        one[...] = jnp.zeros_like(one)
    for span in range(CHIPS):
        at = slice(span * SPAN, (span + 1) * SPAN)
        grad[span] = lax.dot_general(
            weight_ref[at, :], scaled_ref[at, :], TN, preferred_element_type=F32)

    def edge_step(j, carry):
        for r in range(unroll):
            for k, one in enumerate(sums):
                edge = k * SPAN + j * unroll + r
                place = pl.ds(head_ref[edge], 1)
                one[place, :] = one[place, :] + head_grad_ref[pl.ds(edge, 1), :]
        return carry

    lax.fori_loop(0, SPAN // unroll, edge_step, 0)

    def neg_step(j, carry):
        for r in range(unroll):
            for k, one in enumerate(sums):
                place = pl.ds(neg_ref[k * NEG_PAD + j * unroll + r], 1)
                one[place, :] = one[place, :] + grad[k, pl.ds(j * unroll + r, 1), :]
        return carry

    lax.fori_loop(0, negatives // unroll, neg_step, 0)
    total = (a0[0:ROWS, :] + a1[0:ROWS, :]) + (a2[0:ROWS, :] + a3[0:ROWS, :])
    out_ref[...] = total


def owner_kernel(unroll, asked_ref, slope_ref, came_ref, part_ref, out_ref,
                 wide, a0, a1, a2, a3):
    sums = (a0, a1, a2, a3)
    for one in sums[1:]:
        one[...] = jnp.zeros_like(one)
    a0[0:ROWS, :] = part_ref[...]
    a0[ROWS : ROWS + 8, :] = jnp.zeros((8, LANES), F32)
    wide[...] = came_ref[...].astype(F32)
    each = BUCKETS // 4

    def source(s, carry):
        def group(j):
            for r in range(unroll):
                for k, one in enumerate(sums):
                    owner = k * each + s
                    slot = j * unroll + r
                    place = pl.ds(asked_ref[owner * LANES + slot], 1)
                    term = slope_ref[owner * LANES + slot] * wide[pl.ds(owner * LANES + slot, 1), :]
                    one[place, :] = one[place, :] + term
            return j + 1

        def more(j):
            at = jnp.minimum(j * unroll, LANES - 1)
            first = asked_ref[s * LANES + at]
            for k in range(1, 4):
                first = jnp.minimum(first, asked_ref[(k * each + s) * LANES + at])
            return jnp.logical_and(j * unroll < LANES, first < DUMP)

        lax.while_loop(more, group, 0)
        return carry

    lax.fori_loop(0, each, source, 0)
    total = (a0[0:ROWS, :] + a1[0:ROWS, :]) + (a2[0:ROWS, :] + a3[0:ROWS, :])
    out_ref[...] = total


def body(entity_table, relation_table, head_row, relation_id, tail_owner, tail_row, negative_row):
    negatives = negative_row.shape[1]
    place = lax.axis_index("col")
    chip = (place // 2).astype(jnp.int32).reshape(1)
    core = (place % 2).astype(jnp.int32).reshape(1)
    pad = jnp.pad(negative_row, ((0, 0), (0, NEG_PAD - negatives)), constant_values=DUMP)
    pad = pad.reshape(CHIPS * NEG_PAD)
    pack = shape((NEG_PAD + SPAN, LANES), BF16)
    flat = shape((EDGES, LANES), BF16)
    wide = pltpu.VMEM((ROWS + 8, LANES), F32)

    flags = [pltpu.SemaphoreType.DMA] * 2
    lists = (BUCKETS, 1, LANES)
    target, asked = call(
        rank_kernel, "rank", (shape((1, EDGES), jnp.int32), shape(lists, jnp.int32)), [VM, VM],
        [pltpu.VMEM(lists, jnp.int32)] + flags, group=0,
    )(tail_owner.reshape(1, EDGES), tail_row.reshape(1, EDGES))
    asked = asked.reshape(BUCKETS * LANES)
    places = target.reshape(EDGES)

    found = call(
        functools.partial(found_kernel, 32), "found",
        shape((BUCKETS, LANES, LANES), BF16), [SM, VM], [wide], size=15000000,
    )(asked, entity_table)
    fetched = lax.all_to_all(found, "bucket", split_axis=0, concat_axis=0, tiled=True)

    _, head_late = lax.optimization_barrier((found, head_row))
    p0, p1, p2, p3, product, heads, rels, negs = call(
        functools.partial(gather_kernel, 64), "gather",
        (pack, pack, pack, pack, flat, flat, flat, shape((CHIPS, NEG_PAD, LANES), BF16)),
        [SM, SM, SM, SM, VM, VM],
        [wide, pltpu.VMEM((RELS, LANES), F32)], size=30000000,
    )(chip, head_late, relation_id, pad, entity_table, relation_table)

    def along(step):
        return [(2 * x + c, 2 * ((x + step) % CHIPS) + c) for x in range(CHIPS) for c in range(2)]

    q1 = lax.ppermute(p1, "col", along(1))
    q2 = lax.ppermute(p2, "col", along(2))
    q3 = lax.ppermute(p3, "col", along(3))

    half = shape((SPAN // 2, NEG_PAD), F32)
    keep, send = call(score_kernel, "scores", (half, half), [SM, VM, VM, VM, VM],
                      flops=500000000)(core, p0, q1, q2, q3)
    other = lax.ppermute(send, "col", [(c, c ^ 1) for c in range(8)])
    weight, stat = call(
        functools.partial(soft_kernel, negatives), "soft",
        (shape((SPAN // 2, NEG_PAD), BF16), shape((2, SPAN // 2), F32)), [VM, VM],
    )(keep, other)
    weights = lax.all_gather(weight, "col", axis=0, tiled=True)

    tails, partial, slots = call(
        functools.partial(tail_kernel, 32), "tails",
        (flat, shape((1, EDGES), F32), shape((BUCKETS * LANES, LANES), BF16)), [SM, VM, VM],
        [pltpu.VMEM((BUCKETS * LANES, LANES), F32), pltpu.VMEM((BUCKETS * LANES, LANES), F32),
         pltpu.VMEM((EDGES, LANES), F32)], size=15000000,
    )(places, fetched.reshape(BUCKETS * LANES, LANES), product)
    came = lax.all_to_all(slots.reshape(BUCKETS, LANES, LANES), "bucket",
                          split_axis=0, concat_axis=0, tiled=True)
    positive, stats = call(
        functools.partial(share_kernel, 8), "share",
        (shape((1, EDGES), F32), shape((8, 2, SPAN // 2), F32)), [VM, VM],
        [pltpu.VMEM((8, 1, EDGES), F32), pltpu.SemaphoreType.DMA((2,)),
         pltpu.SemaphoreType.DMA((2,))], group=1,
    )(partial, stat)

    loss, head_grad, rel_local, slope, scaled = call(
        functools.partial(edge_kernel, 8), "edges",
        (shape((1, EDGES), F32), shape((EDGES, LANES), F32), shape((RELS, LANES), BF16),
         shape(lists, F32), flat),
        [SM] + [VM] * 9,
        [pltpu.VMEM((EDGES, LANES), F32)] + [pltpu.VMEM((RELS, LANES), F32)] * 4,
        size=20000000,
    )(relation_id, target, positive, stats, weights, negs, product, heads, rels, tails)
    rel_parts = lax.all_to_all(rel_local.reshape(BUCKETS, LANES, LANES), "bucket",
                               split_axis=0, concat_axis=0, tiled=True)
    slopes = call(slope_kernel, "slopes", shape(lists, F32), [VM], flags, group=2)(slope)

    part = call(
        functools.partial(entity_kernel, 8, negatives), "entities", shape((ROWS, LANES), F32),
        [SM, SM, VM, VM, VM],
        [pltpu.VMEM((CHIPS, NEG_PAD, LANES), F32)] + [wide] * 4, size=40000000,
    )(head_row, pad, weights, scaled, head_grad)
    grad = call(
        functools.partial(owner_kernel, 8), "owners", shape((ROWS, LANES), F32),
        [SM, SM, VM, VM],
        [pltpu.VMEM((BUCKETS * LANES, LANES), F32)] + [wide] * 4, size=30000000,
    )(asked, slopes.reshape(BUCKETS * LANES), came.reshape(BUCKETS * LANES, LANES), part)
    relation_grad = jnp.sum(rel_parts.astype(F32), axis=0)
    return (loss.reshape(EDGES), grad, relation_grad)


def solution(mesh):
    in_specs = (
        P("bucket", "col"),
        P(None, "col"),
        P("bucket"),
        P("bucket"),
        P("bucket", None),
        P("bucket"),
        P("bucket", None),
    )
    out_specs = (P("bucket"), P("bucket", "col"), P("bucket", "col"))
    return jax.shard_map(body, mesh=mesh, in_specs=in_specs, out_specs=out_specs, check_vma=False)
```

```python
import functools

import jax
import jax.numpy as jnp
from jax import lax
from jax.experimental import pallas as pl
from jax.experimental.pallas import tpu as pltpu
from jax.sharding import PartitionSpec as P

LANES = 128
SPAN = 512
NEG_PAD = 1024
ROWS = 8192
DUMP = 8192
RELS = 4096
EDGES = 2048
BUCKETS = 32
COLS = 8
UNROLL = 64
CHIPS = 4
F32 = jnp.float32
BF16 = jnp.bfloat16
VM = pl.BlockSpec(memory_space=pltpu.VMEM)
SM = pl.BlockSpec(memory_space=pltpu.SMEM)
NT = (((1,), (1,)), ((), ()))
TN = (((0,), (0,)), ((), ()))


def call(kernel, name, outs, ins, scratch=(), flops=1000000, size=4000000, group=None):
    remote = {} if group is None else dict(collective_id=group, has_side_effects=True)
    return pl.pallas_call(
        kernel,
        name=name,
        out_shape=outs,
        in_specs=ins,
        out_specs=jax.tree.map(lambda _: VM, outs),
        scratch_shapes=scratch,
        compiler_params=pltpu.CompilerParams(vmem_limit_bytes=56 << 20, **remote),
        cost_estimate=pl.CostEstimate(flops=flops, bytes_accessed=size, transcendentals=0),
    )


def shape(dims, kind):
    return jax.ShapeDtypeStruct(dims, kind)


def iota(dims, axis):
    return lax.broadcasted_iota(jnp.int32, dims, axis)


def to_column(row):
    size = row.shape[1]
    same = iota((size, size), 0) == iota((size, size), 1)
    return jnp.sum(jnp.where(same, row, 0.0), axis=1, keepdims=True)


def to_row(column):
    size = column.shape[0]
    same = iota((size, size), 0) == iota((size, size), 1)
    return jnp.sum(jnp.where(same, column, 0.0), axis=0, keepdims=True)


def swap_halves(value):
    return pltpu.roll(value, LANES // 2, 1)


def times(left, right):
    lane = iota(left.shape, 1)
    first = lane < LANES // 2
    turned = swap_halves(right)
    real = jnp.where(first, right, turned)
    imag = jnp.where(first, -turned, right)
    return left * real + swap_halves(left) * imag


def times_conj(left, right):
    lane = iota(left.shape, 1)
    first = lane < LANES // 2
    turned = swap_halves(right)
    real = jnp.where(first, right, turned)
    imag = jnp.where(first, turned, -right)
    return left * real + swap_halves(left) * imag


def greet(axis, count):
    me = lax.axis_index(axis)
    barrier = pltpu.get_barrier_semaphore()

    def tell(i, carry):
        peer = lax.rem(me + i, count)
        pl.semaphore_signal(barrier, inc=1, device_id={axis: peer},
                            device_id_type=pl.DeviceIdType.MESH)
        return carry

    lax.fori_loop(1, count, tell, 0)
    pl.semaphore_wait(barrier, count - 1)


def spread(axis, count, src, dst, send_sem, recv_sem):
    me = lax.axis_index(axis)

    def send(i, carry):
        peer = lax.rem(me + i, count)
        pltpu.make_async_remote_copy(
            src_ref=src.at[peer], dst_ref=dst.at[me], send_sem=send_sem, recv_sem=recv_sem,
            device_id={axis: peer}, device_id_type=pl.DeviceIdType.MESH).start()
        return carry

    lax.fori_loop(1, count, send, 0)


def settle(axis, count, src, dst, send_sem, recv_sem):
    me = lax.axis_index(axis)
    rest = pl.ds(0, count - 1)
    pltpu.make_async_remote_copy(
        src_ref=src.at[rest], dst_ref=dst.at[rest], send_sem=send_sem, recv_sem=recv_sem,
        device_id={axis: lax.rem(me + 1, count)}, device_id_type=pl.DeviceIdType.MESH).wait()


def slope_kernel(slope_ref, out_ref, send_sem, recv_sem):
    greet("bucket", BUCKETS)
    spread("bucket", BUCKETS, slope_ref, out_ref, send_sem, recv_sem)
    me = lax.axis_index("bucket")
    out_ref[me] = slope_ref[me]
    settle("bucket", BUCKETS, slope_ref, out_ref, send_sem, recv_sem)


def load_table(table_ref, wide_ref, rows):
    wide_ref[0:rows, :] = table_ref[...].astype(F32)


def to(peers):
    return dict(device_id=peers, device_id_type=pl.DeviceIdType.MESH)


def forward_kernel(negatives, head_ref, rel_ref, neg_ref, owner_ref, row_ref, table_ref, rtable_ref,
                   target_ref, asked_ref, came_ref, tails_ref, product_ref, heads_ref, rels_ref,
                   negs_ref, weights_ref, stats_ref, positive_ref,
                   wide, rwide, prod_wide, tail_wide, request, inverse, found, fetched, slots,
                   pack, got, keep, send, other, parts, asked_s, target_s, inverse_s,
                   local_sem, bucket_send, bucket_recv, pack_send, pack_recv, swap_send, swap_recv,
                   weight_send, weight_recv, near_send, near_recv, part_send, part_recv):
    me = lax.axis_index("bucket")
    place = lax.axis_index("col")
    chip, core = place // 2, lax.rem(place, 2)
    near = {"col": 2 * chip + (1 - core)}

    barrier = pltpu.get_barrier_semaphore()
    for axis, count in (("bucket", BUCKETS), ("col", COLS)):
        def tell(i, carry):
            peer = lax.rem(lax.axis_index(axis) + i, count)
            pl.semaphore_signal(barrier, inc=1, **to({axis: peer}))
            return carry

        lax.fori_loop(1, count, tell, 0)
    load_table(table_ref, wide, ROWS)
    load_table(rtable_ref, rwide, RELS)
    wide[ROWS : ROWS + 8, :] = jnp.zeros((8, LANES), F32)
    prod_wide[EDGES : EDGES + 8, :] = jnp.zeros((8, LANES), F32)

    def pack_copy(step):
        return pltpu.make_async_remote_copy(
            src_ref=pack.at[step], dst_ref=got.at[step], send_sem=pack_send.at[step],
            recv_sem=pack_recv.at[step], **to({"col": 2 * lax.rem(chip + step, CHIPS) + core}))

    def fill(step):
        span = lax.rem(chip + step, CHIPS)

        def edge_step(j, carry):
            base = pl.multiple_of(span * SPAN + j * UNROLL, UNROLL)
            head = jnp.concatenate(
                [wide[pl.ds(head_ref[base + r], 1), :] for r in range(UNROLL)], axis=0)
            rel = jnp.concatenate(
                [rwide[pl.ds(rel_ref[base + r], 1), :] for r in range(UNROLL)], axis=0)
            product = times(head, rel).astype(BF16)
            at = pl.ds(base, UNROLL)
            pack[step, pl.ds(pl.multiple_of(NEG_PAD + j * UNROLL, UNROLL), UNROLL), :] = product
            product_ref[at, :] = product
            prod_wide[at, :] = product.astype(F32)
            heads_ref[at, :] = head.astype(BF16)
            rels_ref[at, :] = rel.astype(BF16)
            return carry

        lax.fori_loop(0, SPAN // UNROLL, edge_step, 0)

        def neg_step(j, carry):
            base = pl.multiple_of(j * UNROLL, UNROLL)
            start = span * NEG_PAD + j * UNROLL
            rows = jnp.concatenate(
                [wide[pl.ds(neg_ref[start + r], 1), :] for r in range(UNROLL)],
                axis=0).astype(BF16)
            pack[step, pl.ds(base, UNROLL), :] = rows
            negs_ref[span, pl.ds(base, UNROLL), :] = rows
            return carry

        lax.fori_loop(0, NEG_PAD // UNROLL, neg_step, 0)

    fill(2)
    pl.semaphore_wait(barrier, BUCKETS + COLS - 2)

    pack_copy(2).start()
    fill(1)
    pack_copy(1).start()
    fill(3)
    pack_copy(3).start()

    lower = (iota((LANES, LANES), 0) <= iota((LANES, LANES), 1)).astype(BF16)
    lane = iota((LANES, LANES), 1).astype(F32)
    before = jnp.zeros((BUCKETS, 1), F32)
    nothing = jnp.zeros((BUCKETS, LANES), F32)
    high, low, first, last = nothing, nothing, nothing, nothing
    for block in range(EDGES // LANES):
        at = slice(block * LANES, (block + 1) * LANES)
        owner = owner_ref[:, at]
        row = row_ref[:, at]
        mine = iota((BUCKETS, LANES), 0) == owner
        hit = mine.astype(F32).astype(BF16)
        count = jnp.dot(hit, lower, preferred_element_type=F32)
        ranks = jnp.where(mine, count + before - 1.0, 0.0)
        rank = jnp.sum(ranks, axis=0, keepdims=True).astype(jnp.int32)
        before = before + count[:, LANES - 1 : LANES]
        target_ref[block] = jnp.clip(owner * LANES + rank, 0, BUCKETS * LANES - 1)
        slot = iota((LANES, LANES), 0) == rank

        def placed(values):
            spread_out = jnp.where(slot, values, 0.0).astype(BF16)
            return lax.dot_general(hit, spread_out, NT, preferred_element_type=F32)

        high = high + placed((row >> 7).astype(F32))
        low = low + placed((row & 127).astype(F32))
        first = first + float(block) * placed(jnp.ones((1, LANES), F32))
        last = last + placed(lane)
    used = iota((BUCKETS, LANES), 1).astype(F32) < before
    rows = jnp.where(used, high * 128.0 + low, float(DUMP)).astype(jnp.int32)
    edges = jnp.where(used, first * 128.0 + last, float(EDGES)).astype(jnp.int32)
    for owner in range(BUCKETS):
        request[owner] = jnp.clip(rows[owner : owner + 1, :], 0, DUMP)
        inverse[owner] = jnp.clip(edges[owner : owner + 1, :], 0, EDGES)

    spread("bucket", BUCKETS, request, asked_ref, bucket_send.at[0], bucket_recv.at[0])
    copies = [pltpu.make_async_copy(target_ref, target_s, local_sem.at[0]),
              pltpu.make_async_copy(inverse, inverse_s, local_sem.at[1])]
    for copy in copies:
        copy.start()
    asked_ref[me] = request[me]

    fill(0)

    settle("bucket", BUCKETS, request, asked_ref, bucket_send.at[0], bucket_recv.at[0])
    copy = pltpu.make_async_copy(asked_ref, asked_s, local_sem.at[2])
    copy.start()
    copy.wait()

    def bucket_copy(src, dst, which, peer):
        return pltpu.make_async_remote_copy(
            src_ref=src.at[peer], dst_ref=dst.at[me], send_sem=bucket_send.at[which],
            recv_sem=bucket_recv.at[which], **to({"bucket": peer}))

    def take(source, index, out, s):
        for part in range(LANES // UNROLL):
            rows = jnp.concatenate(
                [source[pl.ds(index[s, 0, part * UNROLL + r], 1), :] for r in range(UNROLL)],
                axis=0)
            out[s, part * UNROLL : (part + 1) * UNROLL, :] = rows.astype(BF16)

    def find(i, carry):
        peer = lax.rem(me + i, BUCKETS)
        take(wide, asked_s, found, peer)
        bucket_copy(found, fetched, 1, peer).start()
        return carry

    lax.fori_loop(1, BUCKETS, find, 0)
    take(wide, asked_s, fetched, me)

    for step in range(1, CHIPS):
        pack_copy(step).wait()
    halves = SPAN // 2
    swap = pltpu.make_async_remote_copy(
        src_ref=send, dst_ref=other, send_sem=swap_send, recv_sem=swap_recv, **to(near))

    def score(half, out):
        at = pl.ds(pl.multiple_of(NEG_PAD + half * halves, halves), halves)
        parts_of = [pack.at[0]] + [got.at[step] for step in range(1, CHIPS)]
        left = jnp.concatenate([q[at, :] for q in parts_of], axis=1)

        def piece(i, carry):
            cut = pl.ds(pl.multiple_of(i * 256, 256), 256)
            right = jnp.concatenate([q[cut, :] for q in parts_of], axis=1)
            out[:, cut] = lax.dot_general(left, right, NT, preferred_element_type=F32)
            return carry

        lax.fori_loop(0, NEG_PAD // 256, piece, 0)

    score(1 - core, send)
    swap.start()
    score(core, keep)
    swap.wait()

    for block in range(halves // LANES):
        at = slice(block * LANES, (block + 1) * LANES)
        scores = keep[at, :] + other[at, :]
        real = iota((LANES, NEG_PAD), 1) < negatives
        scores = jnp.where(real, scores, -jnp.inf)
        top = jnp.max(scores, axis=1, keepdims=True)
        expo = jnp.exp(scores - top)
        weights_ref[place, at, :] = expo.astype(BF16)
        stats_ref[place, 0:1, at] = to_row(top)
        stats_ref[place, 1:2, at] = to_row(jnp.sum(expo, axis=1, keepdims=True))

    def weight_copy(step):
        return pltpu.make_async_remote_copy(
            src_ref=weights_ref.at[place], dst_ref=weights_ref.at[place],
            send_sem=weight_send.at[step], recv_sem=weight_recv.at[step],
            **to({"col": 2 * lax.rem(chip + step, CHIPS) + core}))

    def near_copy(step, side):
        piece = 2 * lax.rem(chip - step + CHIPS, CHIPS) + side
        return pltpu.make_async_remote_copy(
            src_ref=weights_ref.at[piece], dst_ref=weights_ref.at[piece],
            send_sem=near_send.at[step], recv_sem=near_recv.at[step], **to(near))

    def weight_came(step):
        piece = 2 * lax.rem(chip - step + CHIPS, CHIPS) + core
        pltpu.make_async_remote_copy(
            src_ref=weights_ref.at[piece], dst_ref=weights_ref.at[piece],
            send_sem=weight_send.at[step], recv_sem=weight_recv.at[step], **to(near)).wait_recv()

    for step in range(1, CHIPS):
        weight_copy(step).start()
    near_copy(0, core).start()

    for copy in copies:
        copy.wait()

    def give(i, carry):
        peer = lax.rem(me + i, BUCKETS)
        take(prod_wide, inverse_s, slots, peer)
        bucket_copy(slots, came_ref, 2, peer).start()
        return carry

    lax.fori_loop(1, BUCKETS, give, 0)
    take(prod_wide, inverse_s, came_ref, me)

    settle("bucket", BUCKETS, found, fetched, bucket_send.at[1], bucket_recv.at[1])
    tail_wide[...] = fetched[...].reshape(BUCKETS * LANES, LANES).astype(F32)

    def tail_step(block, carry):
        base = pl.multiple_of(block * LANES, LANES)
        for part in range(LANES // UNROLL):
            rows = jnp.concatenate(
                [tail_wide[pl.ds(target_s[block, 0, part * UNROLL + r], 1), :]
                 for r in range(UNROLL)], axis=0)
            tails_ref[pl.ds(pl.multiple_of(base + part * UNROLL, UNROLL), UNROLL), :] = (
                rows.astype(BF16))
        at = pl.ds(base, LANES)
        both = tails_ref[at, :].astype(F32) * prod_wide[at, :]
        parts[place, block] = to_row(jnp.sum(both, axis=1, keepdims=True))
        return carry

    lax.fori_loop(0, EDGES // LANES, tail_step, 0)

    def part_copy(k, ref, peer):
        return pltpu.make_async_remote_copy(
            src_ref=ref.at[place], dst_ref=ref.at[place], send_sem=part_send.at[k],
            recv_sem=part_recv.at[k], **to({"col": peer}))

    def tell_parts(i, carry):
        peer = lax.rem(place + i, COLS)
        part_copy(0, parts, peer).start()
        part_copy(1, stats_ref, peer).start()
        return carry

    lax.fori_loop(1, COLS, tell_parts, 0)

    for step in range(1, CHIPS):
        weight_came(step)
        near_copy(step, core).start()
    rest = pl.ds(0, COLS - 1)
    for k, ref in enumerate((parts, stats_ref)):
        pltpu.make_async_remote_copy(
            src_ref=ref.at[rest], dst_ref=ref.at[rest], send_sem=part_send.at[k],
            recv_sem=part_recv.at[k], **to(near)).wait()
    total = parts[0]
    for k in range(1, COLS):
        total = total + parts[k]
    positive_ref[...] = total
    for step in range(CHIPS):
        near_copy(step, core).wait_send()
        near_copy(step, 1 - core).wait_recv()
    for step in range(1, CHIPS):
        weight_copy(step).wait_send()
    settle("bucket", BUCKETS, slots, came_ref, bucket_send.at[2], bucket_recv.at[2])


def edge_kernel(unroll, rel_ref, target_ref, positive_ref, stat_ref, weight_ref, negs_ref,
                product_ref, heads_ref, rels_ref, tails_ref,
                loss_ref, head_grad_ref, rel_grad_ref, slot_ref, scaled_ref,
                grad, a0, a1, a2, a3):
    sums = (a0, a1, a2, a3)
    for one in sums:
        one[...] = jnp.zeros_like(one)
    slots = jnp.zeros((BUCKETS, LANES), F32)
    half = SPAN // 2
    for block in range(EDGES // LANES):
        at = slice(block * LANES, (block + 1) * LANES)
        part, inner = block // 2, (block % 2) * LANES
        high = stat_ref[part, 0:1, inner : inner + LANES]
        mass = stat_ref[part, 1:2, inner : inner + LANES]
        positive = positive_ref[block]
        top = jnp.maximum(high, positive)
        shrink = jnp.exp(high - top)
        expo = jnp.exp(positive - top)
        total = mass * shrink + expo
        scale = shrink / total
        slope = expo / total - 1.0
        loss_ref[:, at] = top + jnp.log(total) - positive
        target = target_ref[block]
        hit = (iota((BUCKETS, LANES), 0) == (target >> 7)).astype(F32).astype(BF16)
        slot = iota((LANES, LANES), 0) == (target & 127)
        rest = slope
        for _ in range(3):
            piece = rest.astype(BF16)
            spread = jnp.where(slot, piece.astype(F32), 0.0).astype(BF16)
            slots = slots + lax.dot_general(hit, spread, NT, preferred_element_type=F32)
            rest = rest - piece.astype(F32)
        scale_col = to_column(scale)
        slope_col = to_column(slope)
        scaled_ref[at, :] = (product_ref[at, :].astype(F32) * scale_col).astype(BF16)
        raw = jnp.dot(weight_ref[at, :], negs_ref[block // 4], preferred_element_type=F32)
        down = raw * scale_col + slope_col * tails_ref[at, :].astype(F32)
        head_grad_ref[at, :] = times_conj(down, rels_ref[at, :].astype(F32))
        grad[at, :] = times_conj(down, heads_ref[at, :].astype(F32))
    for owner in range(BUCKETS):
        slot_ref[owner] = slots[owner : owner + 1, :]

    def step(j, carry):
        for r in range(unroll):
            for k, one in enumerate(sums):
                edge = k * SPAN + j * unroll + r
                place = pl.ds(rel_ref[edge], 1)
                one[place, :] = one[place, :] + grad[pl.ds(edge, 1), :]
        return carry

    lax.fori_loop(0, SPAN // unroll, step, 0)
    rel_grad_ref[...] = ((a0[...] + a1[...]) + (a2[...] + a3[...])).astype(BF16)


def entity_kernel(unroll, negatives, head_ref, neg_ref, weight_ref, scaled_ref, head_grad_ref,
                  out_ref, grad, a0, a1, a2, a3):
    sums = (a0, a1, a2, a3)
    for one in sums:
        one[...] = jnp.zeros_like(one)
    for span in range(CHIPS):
        at = slice(span * SPAN, (span + 1) * SPAN)
        grad[span] = lax.dot_general(
            weight_ref[at, :], scaled_ref[at, :], TN, preferred_element_type=F32)

    def edge_step(j, carry):
        for r in range(unroll):
            for k, one in enumerate(sums):
                edge = k * SPAN + j * unroll + r
                place = pl.ds(head_ref[edge], 1)
                one[place, :] = one[place, :] + head_grad_ref[pl.ds(edge, 1), :]
        return carry

    lax.fori_loop(0, SPAN // unroll, edge_step, 0)

    def neg_step(j, carry):
        for r in range(unroll):
            for k, one in enumerate(sums):
                place = pl.ds(neg_ref[k * NEG_PAD + j * unroll + r], 1)
                one[place, :] = one[place, :] + grad[k, pl.ds(j * unroll + r, 1), :]
        return carry

    lax.fori_loop(0, negatives // unroll, neg_step, 0)
    total = (a0[0:ROWS, :] + a1[0:ROWS, :]) + (a2[0:ROWS, :] + a3[0:ROWS, :])
    out_ref[...] = total


def owner_kernel(unroll, asked_ref, slope_ref, came_ref, part_ref, out_ref,
                 wide, a0, a1, a2, a3):
    sums = (a0, a1, a2, a3)
    for one in sums[1:]:
        one[...] = jnp.zeros_like(one)
    a0[0:ROWS, :] = part_ref[...]
    a0[ROWS : ROWS + 8, :] = jnp.zeros((8, LANES), F32)
    wide[...] = came_ref[...].astype(F32)
    each = BUCKETS // 4

    def source(s, carry):
        def group(j):
            for r in range(unroll):
                for k, one in enumerate(sums):
                    owner = k * each + s
                    slot = j * unroll + r
                    place = pl.ds(asked_ref[owner * LANES + slot], 1)
                    term = slope_ref[owner * LANES + slot] * wide[pl.ds(owner * LANES + slot, 1), :]
                    one[place, :] = one[place, :] + term
            return j + 1

        def more(j):
            at = jnp.minimum(j * unroll, LANES - 1)
            first = asked_ref[s * LANES + at]
            for k in range(1, 4):
                first = jnp.minimum(first, asked_ref[(k * each + s) * LANES + at])
            return jnp.logical_and(j * unroll < LANES, first < DUMP)

        lax.while_loop(more, group, 0)
        return carry

    lax.fori_loop(0, each, source, 0)
    total = (a0[0:ROWS, :] + a1[0:ROWS, :]) + (a2[0:ROWS, :] + a3[0:ROWS, :])
    out_ref[...] = total


def body(entity_table, relation_table, head_row, relation_id, tail_owner, tail_row, negative_row):
    negatives = negative_row.shape[1]
    pad = jnp.pad(negative_row, ((0, 0), (0, NEG_PAD - negatives)), constant_values=DUMP)
    pad = pad.reshape(CHIPS * NEG_PAD)
    flat = shape((EDGES, LANES), BF16)
    wide = pltpu.VMEM((ROWS + 8, LANES), F32)
    lists = (BUCKETS, 1, LANES)
    blocks = (EDGES // LANES, 1, LANES)
    grid = (BUCKETS, LANES, LANES)
    half = pltpu.VMEM((SPAN // 2, NEG_PAD), F32)
    packs = pltpu.VMEM((CHIPS, NEG_PAD + SPAN, LANES), BF16)
    flag = pltpu.SemaphoreType.DMA
    (target, asked, came, tails, product, heads, rels, negs, weights, stats, positive) = call(
        functools.partial(forward_kernel, negatives), "forward",
        (shape(blocks, jnp.int32), shape(lists, jnp.int32), shape(grid, BF16), flat, flat, flat,
         flat, shape((CHIPS, NEG_PAD, LANES), BF16), shape((COLS, SPAN // 2, NEG_PAD), BF16),
         shape((COLS, 2, SPAN // 2), F32), shape(blocks, F32)),
        [SM] * 3 + [VM] * 4,
        [wide, pltpu.VMEM((RELS, LANES), F32), pltpu.VMEM((EDGES + 8, LANES), F32),
         pltpu.VMEM((BUCKETS * LANES, LANES), F32), pltpu.VMEM(lists, jnp.int32),
         pltpu.VMEM(lists, jnp.int32), pltpu.VMEM(grid, BF16), pltpu.VMEM(grid, BF16),
         pltpu.VMEM(grid, BF16), packs, packs, half, half, half,
         pltpu.VMEM((COLS,) + blocks, F32), pltpu.SMEM(lists, jnp.int32),
         pltpu.SMEM(blocks, jnp.int32), pltpu.SMEM(lists, jnp.int32),
         flag((3,)), flag((3,)), flag((3,)), flag((CHIPS,)), flag((CHIPS,)), flag, flag,
         flag((CHIPS,)), flag((CHIPS,)), flag((CHIPS,)), flag((CHIPS,)), flag((2,)), flag((2,))],
        flops=600000000, size=40000000, group=0,
    )(head_row, relation_id, pad, tail_owner.reshape(1, EDGES), tail_row.reshape(1, EDGES),
      entity_table, relation_table)
    asked = asked.reshape(BUCKETS * LANES)
    weights = weights.reshape(EDGES, NEG_PAD)
    flags = [flag] * 2

    loss, head_grad, rel_local, slope, scaled = call(
        functools.partial(edge_kernel, 8), "edges",
        (shape((1, EDGES), F32), shape((EDGES, LANES), F32), shape((RELS, LANES), BF16),
         shape(lists, F32), flat),
        [SM] + [VM] * 9,
        [pltpu.VMEM((EDGES, LANES), F32)] + [pltpu.VMEM((RELS, LANES), F32)] * 4,
        size=20000000,
    )(relation_id, target, positive, stats, weights, negs, product, heads, rels, tails)
    slopes = call(slope_kernel, "slopes", shape(lists, F32), [VM], flags, group=1)(slope)
    _, rel_local = lax.optimization_barrier((slopes, rel_local))
    rel_parts = lax.all_to_all(rel_local.reshape(BUCKETS, LANES, LANES), "bucket",
                               split_axis=0, concat_axis=0, tiled=True)

    part = call(
        functools.partial(entity_kernel, 8, negatives), "entities", shape((ROWS, LANES), F32),
        [SM, SM, VM, VM, VM],
        [pltpu.VMEM((CHIPS, NEG_PAD, LANES), F32)] + [wide] * 4, size=40000000,
    )(head_row, pad, weights, scaled, head_grad)
    grad = call(
        functools.partial(owner_kernel, 8), "owners", shape((ROWS, LANES), F32),
        [SM, SM, VM, VM],
        [pltpu.VMEM((BUCKETS * LANES, LANES), F32)] + [wide] * 4, size=30000000,
    )(asked, slopes.reshape(BUCKETS * LANES), came.reshape(BUCKETS * LANES, LANES), part)
    relation_grad = jnp.sum(rel_parts.astype(F32), axis=0)
    return (loss.reshape(EDGES), grad, relation_grad)


def solution(mesh):
    in_specs = (
        P("bucket", "col"),
        P(None, "col"),
        P("bucket"),
        P("bucket"),
        P("bucket", None),
        P("bucket"),
        P("bucket", None),
    )
    out_specs = (P("bucket"), P("bucket", "col"), P("bucket", "col"))
    return jax.shard_map(body, mesh=mesh, in_specs=in_specs, out_specs=out_specs, check_vma=False)
```

```python
import functools

import jax
import jax.numpy as jnp
from jax import lax
from jax.experimental import pallas as pl
from jax.experimental.pallas import tpu as pltpu
from jax.sharding import PartitionSpec as P

LANES = 128
SPAN = 512
NEG_PAD = 1024
ROWS = 8192
DUMP = 8192
RELS = 4096
EDGES = 2048
BUCKETS = 32
COLS = 8
UNROLL = 64
CHIPS = 4
F32 = jnp.float32
BF16 = jnp.bfloat16
VM = pl.BlockSpec(memory_space=pltpu.VMEM)
SM = pl.BlockSpec(memory_space=pltpu.SMEM)
NT = (((1,), (1,)), ((), ()))
TN = (((0,), (0,)), ((), ()))


def call(kernel, name, outs, ins, scratch=(), flops=1000000, size=4000000, group=None):
    remote = {} if group is None else dict(collective_id=group, has_side_effects=True)
    return pl.pallas_call(
        kernel,
        name=name,
        out_shape=outs,
        in_specs=ins,
        out_specs=jax.tree.map(lambda _: VM, outs),
        scratch_shapes=scratch,
        compiler_params=pltpu.CompilerParams(vmem_limit_bytes=56 << 20, **remote),
        cost_estimate=pl.CostEstimate(flops=flops, bytes_accessed=size, transcendentals=0),
    )


def shape(dims, kind):
    return jax.ShapeDtypeStruct(dims, kind)


def iota(dims, axis):
    return lax.broadcasted_iota(jnp.int32, dims, axis)


def to_column(row):
    size = row.shape[1]
    same = iota((size, size), 0) == iota((size, size), 1)
    return jnp.sum(jnp.where(same, row, 0.0), axis=1, keepdims=True)


def to_row(column):
    size = column.shape[0]
    same = iota((size, size), 0) == iota((size, size), 1)
    return jnp.sum(jnp.where(same, column, 0.0), axis=0, keepdims=True)


def swap_halves(value):
    return pltpu.roll(value, LANES // 2, 1)


def times(left, right):
    lane = iota(left.shape, 1)
    first = lane < LANES // 2
    turned = swap_halves(right)
    real = jnp.where(first, right, turned)
    imag = jnp.where(first, -turned, right)
    return left * real + swap_halves(left) * imag


def times_conj(left, right):
    lane = iota(left.shape, 1)
    first = lane < LANES // 2
    turned = swap_halves(right)
    real = jnp.where(first, right, turned)
    imag = jnp.where(first, turned, -right)
    return left * real + swap_halves(left) * imag


def greet(axis, count):
    me = lax.axis_index(axis)
    barrier = pltpu.get_barrier_semaphore()

    def tell(i, carry):
        peer = lax.rem(me + i, count)
        pl.semaphore_signal(barrier, inc=1, device_id={axis: peer},
                            device_id_type=pl.DeviceIdType.MESH)
        return carry

    lax.fori_loop(1, count, tell, 0)
    pl.semaphore_wait(barrier, count - 1)


def spread(axis, count, src, dst, send_sem, recv_sem):
    me = lax.axis_index(axis)

    def send(i, carry):
        peer = lax.rem(me + i, count)
        pltpu.make_async_remote_copy(
            src_ref=src.at[peer], dst_ref=dst.at[me], send_sem=send_sem, recv_sem=recv_sem,
            device_id={axis: peer}, device_id_type=pl.DeviceIdType.MESH).start()
        return carry

    lax.fori_loop(1, count, send, 0)


def settle(axis, count, src, dst, send_sem, recv_sem):
    me = lax.axis_index(axis)
    rest = pl.ds(0, count - 1)
    pltpu.make_async_remote_copy(
        src_ref=src.at[rest], dst_ref=dst.at[rest], send_sem=send_sem, recv_sem=recv_sem,
        device_id={axis: lax.rem(me + 1, count)}, device_id_type=pl.DeviceIdType.MESH).wait()


def load_table(table_ref, wide_ref, rows):
    wide_ref[0:rows, :] = table_ref[...].astype(F32)


def to(peers):
    return dict(device_id=peers, device_id_type=pl.DeviceIdType.MESH)


def forward_kernel(negatives, head_ref, rel_ref, neg_ref, owner_ref, row_ref, table_ref, rtable_ref,
                   asked_ref, came_ref, slopes_ref, loss_ref, head_grad_ref, rel_grad_ref,
                   neg_grad_ref,
                   wide, rwide, prod_wide, heads, rels, tails, raw, scaled, weights, tail_wide,
                   target, request, inverse, found, fetched, slots, pack, got, keep, send, other,
                   parts, stats, slope_out, asked_s, target_s, inverse_s,
                   local_sem, bucket_send, bucket_recv, pack_send, pack_recv, swap_send, swap_recv,
                   weight_send, weight_recv, near_send, near_recv, part_send, part_recv):
    me = lax.axis_index("bucket")
    place = lax.axis_index("col")
    chip, core = place // 2, lax.rem(place, 2)
    near = {"col": 2 * chip + (1 - core)}

    barrier = pltpu.get_barrier_semaphore()
    for axis, count in (("bucket", BUCKETS), ("col", COLS)):
        def tell(i, carry):
            peer = lax.rem(lax.axis_index(axis) + i, count)
            pl.semaphore_signal(barrier, inc=1, **to({axis: peer}))
            return carry

        lax.fori_loop(1, count, tell, 0)
    lower = (iota((LANES, LANES), 0) <= iota((LANES, LANES), 1)).astype(BF16)
    lane = iota((LANES, LANES), 1).astype(F32)
    before = jnp.zeros((BUCKETS, 1), F32)
    nothing = jnp.zeros((BUCKETS, LANES), F32)
    high, low, first, last = nothing, nothing, nothing, nothing
    for block in range(EDGES // LANES):
        at = slice(block * LANES, (block + 1) * LANES)
        owner = owner_ref[:, at]
        row = row_ref[:, at]
        mine = iota((BUCKETS, LANES), 0) == owner
        hit = mine.astype(F32).astype(BF16)
        count = jnp.dot(hit, lower, preferred_element_type=F32)
        ranks = jnp.where(mine, count + before - 1.0, 0.0)
        rank = jnp.sum(ranks, axis=0, keepdims=True).astype(jnp.int32)
        before = before + count[:, LANES - 1 : LANES]
        target[block] = jnp.clip(owner * LANES + rank, 0, BUCKETS * LANES - 1)
        slot = iota((LANES, LANES), 0) == rank

        def placed(values):
            spread_out = jnp.where(slot, values, 0.0).astype(BF16)
            return lax.dot_general(hit, spread_out, NT, preferred_element_type=F32)

        high = high + placed((row >> 7).astype(F32))
        low = low + placed((row & 127).astype(F32))
        first = first + float(block) * placed(jnp.ones((1, LANES), F32))
        last = last + placed(lane)
    used = iota((BUCKETS, LANES), 1).astype(F32) < before
    rows = jnp.where(used, high * 128.0 + low, float(DUMP)).astype(jnp.int32)
    edges = jnp.where(used, first * 128.0 + last, float(EDGES)).astype(jnp.int32)
    for owner in range(BUCKETS):
        request[owner] = jnp.clip(rows[owner : owner + 1, :], 0, DUMP)
        inverse[owner] = jnp.clip(edges[owner : owner + 1, :], 0, EDGES)

    pl.semaphore_wait(barrier, BUCKETS + COLS - 2)
    spread("bucket", BUCKETS, request, asked_ref, bucket_send.at[0], bucket_recv.at[0])
    copies = [pltpu.make_async_copy(target, target_s, local_sem.at[0]),
              pltpu.make_async_copy(inverse, inverse_s, local_sem.at[1])]
    for copy in copies:
        copy.start()
    asked_ref[me] = request[me]

    load_table(table_ref, wide, ROWS)
    load_table(rtable_ref, rwide, RELS)
    wide[ROWS : ROWS + 8, :] = jnp.zeros((8, LANES), F32)
    prod_wide[EDGES : EDGES + 8, :] = jnp.zeros((8, LANES), F32)

    def pack_copy(step):
        return pltpu.make_async_remote_copy(
            src_ref=pack.at[step], dst_ref=got.at[step], send_sem=pack_send.at[step],
            recv_sem=pack_recv.at[step], **to({"col": 2 * lax.rem(chip + step, CHIPS) + core}))

    def fill(step):
        span = lax.rem(chip + step, CHIPS)

        def edge_step(j, carry):
            base = pl.multiple_of(span * SPAN + j * UNROLL, UNROLL)
            head = jnp.concatenate(
                [wide[pl.ds(head_ref[base + r], 1), :] for r in range(UNROLL)], axis=0)
            rel = jnp.concatenate(
                [rwide[pl.ds(rel_ref[base + r], 1), :] for r in range(UNROLL)], axis=0)
            product = times(head, rel).astype(BF16)
            at = pl.ds(base, UNROLL)
            pack[step, pl.ds(pl.multiple_of(NEG_PAD + j * UNROLL, UNROLL), UNROLL), :] = product
            prod_wide[at, :] = product.astype(F32)
            heads[at, :] = head
            rels[at, :] = rel
            return carry

        lax.fori_loop(0, SPAN // UNROLL, edge_step, 0)

        def neg_step(j, carry):
            base = pl.multiple_of(j * UNROLL, UNROLL)
            start = span * NEG_PAD + j * UNROLL
            rows = jnp.concatenate(
                [wide[pl.ds(neg_ref[start + r], 1), :] for r in range(UNROLL)],
                axis=0).astype(BF16)
            pack[step, pl.ds(base, UNROLL), :] = rows
            return carry

        lax.fori_loop(0, NEG_PAD // UNROLL, neg_step, 0)

    fill(2)
    pack_copy(2).start()
    fill(1)
    pack_copy(1).start()
    settle("bucket", BUCKETS, request, asked_ref, bucket_send.at[0], bucket_recv.at[0])
    copy = pltpu.make_async_copy(asked_ref, asked_s, local_sem.at[2])
    copy.start()
    copy.wait()

    def bucket_copy(src, dst, which, peer):
        return pltpu.make_async_remote_copy(
            src_ref=src.at[peer], dst_ref=dst.at[me], send_sem=bucket_send.at[which],
            recv_sem=bucket_recv.at[which], **to({"bucket": peer}))

    def take(source, index, out, s):
        for part in range(LANES // UNROLL):
            rows = jnp.concatenate(
                [source[pl.ds(index[s, 0, part * UNROLL + r], 1), :] for r in range(UNROLL)],
                axis=0)
            out[s, part * UNROLL : (part + 1) * UNROLL, :] = rows.astype(BF16)

    def find(i, carry):
        peer = lax.rem(me + i, BUCKETS)
        take(wide, asked_s, found, peer)
        bucket_copy(found, fetched, 1, peer).start()
        return carry

    lax.fori_loop(1, BUCKETS, find, 0)
    take(wide, asked_s, fetched, me)

    fill(3)
    pack_copy(3).start()

    fill(0)

    for copy in copies:
        copy.wait()

    def give(i, carry):
        peer = lax.rem(me + i, BUCKETS)
        take(prod_wide, inverse_s, slots, peer)
        bucket_copy(slots, came_ref, 2, peer).start()
        return carry

    lax.fori_loop(1, BUCKETS, give, 0)
    take(prod_wide, inverse_s, came_ref, me)

    for step in range(1, CHIPS):
        pack_copy(step).wait()
    halves = SPAN // 2

    def swap(block):
        at = pl.ds(block * LANES, LANES)
        return pltpu.make_async_remote_copy(
            src_ref=send.at[at], dst_ref=other.at[at], send_sem=swap_send.at[block],
            recv_sem=swap_recv.at[block], **to(near))

    def score(half, out, block):
        at = pl.ds(pl.multiple_of(NEG_PAD + half * halves + block * LANES, LANES), LANES)
        parts_of = [pack.at[0]] + [got.at[step] for step in range(1, CHIPS)]
        left = jnp.concatenate([q[at, :] for q in parts_of], axis=1)

        def piece(i, carry):
            cut = pl.ds(pl.multiple_of(i * 256, 256), 256)
            right = jnp.concatenate([q[cut, :] for q in parts_of], axis=1)
            out[block * LANES : (block + 1) * LANES, cut] = lax.dot_general(
                left, right, NT, preferred_element_type=F32)
            return carry

        lax.fori_loop(0, NEG_PAD // 256, piece, 0)

    def source(step, side):
        return 2 * lax.rem(chip - step + CHIPS, CHIPS) + side

    def weight_copy(step, block, piece):
        ref = weights.at[piece, pl.ds(block * LANES, LANES)]
        flag = step * 2 + block
        return pltpu.make_async_remote_copy(
            src_ref=ref, dst_ref=ref, send_sem=weight_send.at[flag],
            recv_sem=weight_recv.at[flag],
            **to({"col": 2 * lax.rem(chip + step, CHIPS) + core}))

    def near_copy(step, block, side):
        ref = weights.at[source(step, side), pl.ds(block * LANES, LANES)]
        flag = step * 2 + block
        return pltpu.make_async_remote_copy(
            src_ref=ref, dst_ref=ref, send_sem=near_send.at[flag], recv_sem=near_recv.at[flag],
            **to(near))

    def blend(step, block, side):
        piece = source(step, side)
        at = pl.ds(pl.multiple_of(piece * halves + block * LANES, LANES), LANES)
        raw[at, :] = jnp.dot(weights[piece, block * LANES : (block + 1) * LANES, :],
                             pack[(CHIPS - step) % CHIPS, 0:NEG_PAD, :],
                             preferred_element_type=F32)

    for block in range(2):
        score(1 - core, send, block)
        swap(block).start()
    for block in range(2):
        score(core, keep, block)
    for block in range(2):
        swap(block).wait()
        at = slice(block * LANES, (block + 1) * LANES)
        scores = keep[at, :] + other[at, :]
        real = iota((LANES, NEG_PAD), 1) < negatives
        scores = jnp.where(real, scores, -jnp.inf)
        top = jnp.max(scores, axis=1, keepdims=True)
        expo = jnp.exp(scores - top)
        weights[place, at, :] = expo.astype(BF16)
        for step in (2, 1, 3):
            weight_copy(step, block, place).start()
        near_copy(0, block, core).start()
        stats[place, 0:1, at] = to_row(top)
        stats[place, 1:2, at] = to_row(jnp.sum(expo, axis=1, keepdims=True))

    settle("bucket", BUCKETS, found, fetched, bucket_send.at[1], bucket_recv.at[1])
    tail_wide[...] = fetched[...].reshape(BUCKETS * LANES, LANES).astype(F32)

    def tail_step(block, carry):
        base = pl.multiple_of(block * LANES, LANES)
        for part in range(LANES // UNROLL):
            rows = jnp.concatenate(
                [tail_wide[pl.ds(target_s[block, 0, part * UNROLL + r], 1), :]
                 for r in range(UNROLL)], axis=0)
            tails[pl.ds(pl.multiple_of(base + part * UNROLL, UNROLL), UNROLL), :] = rows
        at = pl.ds(base, LANES)
        both = tails[at, :] * prod_wide[at, :]
        parts[place, block] = to_row(jnp.sum(both, axis=1, keepdims=True))
        return carry

    lax.fori_loop(0, EDGES // LANES, tail_step, 0)

    def part_copy(k, ref, peer):
        return pltpu.make_async_remote_copy(
            src_ref=ref.at[place], dst_ref=ref.at[place], send_sem=part_send.at[k],
            recv_sem=part_recv.at[k], **to({"col": peer}))

    def tell_parts(i, carry):
        peer = lax.rem(place + i, COLS)
        part_copy(0, parts, peer).start()
        part_copy(1, stats, peer).start()
        return carry

    lax.fori_loop(1, COLS, tell_parts, 0)

    for block in range(2):
        blend(0, block, core)
    for block in range(2):
        near_copy(0, block, 1 - core).wait_recv()
        blend(0, block, 1 - core)
    for block in range(2):
        for step in (1, 3, 2):
            weight_copy(step, block, source(step, core)).wait_recv()
            near_copy(step, block, core).start()
            blend(step, block, core)
    rest = pl.ds(0, COLS - 1)
    for k, ref in enumerate((parts, stats)):
        pltpu.make_async_remote_copy(
            src_ref=ref.at[rest], dst_ref=ref.at[rest], send_sem=part_send.at[k],
            recv_sem=part_recv.at[k], **to(near)).wait()

    mass_of, slope_of = [], []
    deal = jnp.zeros((BUCKETS, LANES), F32)
    for block in range(EDGES // LANES):
        part, inner = block // 2, (block % 2) * LANES
        high = stats[part, 0:1, inner : inner + LANES]
        mass = stats[part, 1:2, inner : inner + LANES]
        positive = parts[0, block]
        for k in range(1, COLS):
            positive = positive + parts[k, block]
        top = jnp.maximum(high, positive)
        shrink = jnp.exp(high - top)
        expo = jnp.exp(positive - top)
        total = mass * shrink + expo
        slope = expo / total - 1.0
        loss_ref[block] = top + jnp.log(total) - positive
        mass_of.append(shrink / total)
        slope_of.append(slope)
        goal = target[block]
        hit = (iota((BUCKETS, LANES), 0) == (goal >> 7)).astype(F32).astype(BF16)
        slot = iota((LANES, LANES), 0) == (goal & 127)
        left_over = slope
        for _ in range(3):
            piece = left_over.astype(BF16)
            spread_out = jnp.where(slot, piece.astype(F32), 0.0).astype(BF16)
            deal = deal + lax.dot_general(hit, spread_out, NT, preferred_element_type=F32)
            left_over = left_over - piece.astype(F32)
    for owner in range(BUCKETS):
        slope_out[owner] = deal[owner : owner + 1, :]
    spread("bucket", BUCKETS, slope_out, slopes_ref, bucket_send.at[3], bucket_recv.at[3])
    slopes_ref[me] = slope_out[me]

    for block in range(2):
        for step in (1, 3, 2):
            near_copy(step, block, 1 - core).wait_recv()
            blend(step, block, 1 - core)
    for block in range(EDGES // LANES):
        at = slice(block * LANES, (block + 1) * LANES)
        scale = to_column(mass_of[block])
        scaled[at, :] = (prod_wide[at, :] * scale).astype(BF16)
        down = raw[at, :] * scale + to_column(slope_of[block]) * tails[at, :]
        head_grad_ref[at, :] = times_conj(down, rels[at, :])
        rel_grad_ref[at, :] = times_conj(down, heads[at, :])
    for span in range(CHIPS):
        total = jnp.zeros((NEG_PAD, LANES), F32)
        for side in range(2):
            piece = 2 * span + side
            total = total + lax.dot_general(
                weights[piece], scaled[piece * halves : (piece + 1) * halves, :], TN,
                preferred_element_type=F32)
        neg_grad_ref[span] = total
    for block in range(2):
        for step in range(CHIPS):
            near_copy(step, block, core).wait_send()
        for step in range(1, CHIPS):
            weight_copy(step, block, place).wait_send()
    settle("bucket", BUCKETS, slope_out, slopes_ref, bucket_send.at[3], bucket_recv.at[3])
    settle("bucket", BUCKETS, slots, came_ref, bucket_send.at[2], bucket_recv.at[2])


def relation_kernel(unroll, rel_ref, grad_ref, out_ref, a0, a1, a2, a3):
    sums = (a0, a1, a2, a3)
    for one in sums:
        one[...] = jnp.zeros_like(one)

    def step(j, carry):
        for r in range(unroll):
            for k, one in enumerate(sums):
                edge = k * SPAN + j * unroll + r
                place = pl.ds(rel_ref[edge], 1)
                one[place, :] = one[place, :] + grad_ref[pl.ds(edge, 1), :]
        return carry

    lax.fori_loop(0, SPAN // unroll, step, 0)
    out_ref[...] = ((a0[...] + a1[...]) + (a2[...] + a3[...])).astype(BF16)


def entity_kernel(unroll, negatives, head_ref, neg_ref, asked_ref, slope_ref, head_grad_ref,
                  neg_grad_ref, came_ref, out_ref, wide, a0, a1, a2, a3):
    sums = (a0, a1, a2, a3)
    for one in sums:
        one[...] = jnp.zeros_like(one)
    wide[...] = came_ref[...].astype(F32)

    def edge_step(j, carry):
        for r in range(unroll):
            for k, one in enumerate(sums):
                edge = k * SPAN + j * unroll + r
                place = pl.ds(head_ref[edge], 1)
                one[place, :] = one[place, :] + head_grad_ref[pl.ds(edge, 1), :]
        return carry

    lax.fori_loop(0, SPAN // unroll, edge_step, 0)

    def neg_step(j, carry):
        for r in range(unroll):
            for k, one in enumerate(sums):
                place = pl.ds(neg_ref[k * NEG_PAD + j * unroll + r], 1)
                one[place, :] = one[place, :] + neg_grad_ref[k, pl.ds(j * unroll + r, 1), :]
        return carry

    lax.fori_loop(0, negatives // unroll, neg_step, 0)
    each = BUCKETS // 4

    def source(s, carry):
        def group(j):
            for r in range(unroll):
                for k, one in enumerate(sums):
                    owner = k * each + s
                    slot = j * unroll + r
                    place = pl.ds(asked_ref[owner * LANES + slot], 1)
                    term = slope_ref[owner * LANES + slot] * wide[pl.ds(owner * LANES + slot, 1), :]
                    one[place, :] = one[place, :] + term
            return j + 1

        def more(j):
            at = jnp.minimum(j * unroll, LANES - 1)
            first = asked_ref[s * LANES + at]
            for k in range(1, 4):
                first = jnp.minimum(first, asked_ref[(k * each + s) * LANES + at])
            return jnp.logical_and(j * unroll < LANES, first < DUMP)

        lax.while_loop(more, group, 0)
        return carry

    lax.fori_loop(0, each, source, 0)
    total = (a0[0:ROWS, :] + a1[0:ROWS, :]) + (a2[0:ROWS, :] + a3[0:ROWS, :])
    out_ref[...] = total


def body(entity_table, relation_table, head_row, relation_id, tail_owner, tail_row, negative_row):
    negatives = negative_row.shape[1]
    pad = jnp.pad(negative_row, ((0, 0), (0, NEG_PAD - negatives)), constant_values=DUMP)
    pad = pad.reshape(CHIPS * NEG_PAD)
    wide = pltpu.VMEM((ROWS + 8, LANES), F32)
    lists = (BUCKETS, 1, LANES)
    blocks = (EDGES // LANES, 1, LANES)
    grid = (BUCKETS, LANES, LANES)
    half = pltpu.VMEM((SPAN // 2, NEG_PAD), F32)
    packs = pltpu.VMEM((CHIPS, NEG_PAD + SPAN, LANES), BF16)
    flag = pltpu.SemaphoreType.DMA
    flat32 = pltpu.VMEM((EDGES, LANES), F32)
    asked, came, slopes, loss, head_grad, rel_grad, neg_grad = call(
        functools.partial(forward_kernel, negatives), "forward",
        (shape(lists, jnp.int32), shape(grid, BF16), shape(lists, F32), shape(blocks, F32),
         shape((EDGES, LANES), F32), shape((EDGES, LANES), F32),
         shape((CHIPS, NEG_PAD, LANES), F32)),
        [SM] * 3 + [VM] * 4,
        [wide, pltpu.VMEM((RELS, LANES), F32), pltpu.VMEM((EDGES + 8, LANES), F32),
         flat32, flat32, flat32, flat32, pltpu.VMEM((EDGES, LANES), BF16),
         pltpu.VMEM((COLS, SPAN // 2, NEG_PAD), BF16),
         pltpu.VMEM((BUCKETS * LANES, LANES), F32), pltpu.VMEM(blocks, jnp.int32),
         pltpu.VMEM(lists, jnp.int32), pltpu.VMEM(lists, jnp.int32),
         pltpu.VMEM(grid, BF16), pltpu.VMEM(grid, BF16), pltpu.VMEM(grid, BF16),
         packs, packs, half, half, half,
         pltpu.VMEM((COLS,) + blocks, F32), pltpu.VMEM((COLS, 2, SPAN // 2), F32),
         pltpu.VMEM(lists, F32), pltpu.SMEM(lists, jnp.int32),
         pltpu.SMEM(blocks, jnp.int32), pltpu.SMEM(lists, jnp.int32),
         flag((3,)), flag((4,)), flag((4,)), flag((CHIPS,)), flag((CHIPS,)), flag((2,)),
         flag((2,)), flag((2 * CHIPS,)), flag((2 * CHIPS,)), flag((2 * CHIPS,)),
         flag((2 * CHIPS,)), flag((2,)), flag((2,))],
        flops=600000000, size=40000000, group=0,
    )(head_row, relation_id, pad, tail_owner.reshape(1, EDGES), tail_row.reshape(1, EDGES),
      entity_table, relation_table)

    rel_local = call(
        functools.partial(relation_kernel, 8), "relations", shape((RELS, LANES), BF16),
        [SM, VM], [pltpu.VMEM((RELS, LANES), F32)] * 4, size=10000000,
    )(relation_id, rel_grad)
    rel_parts = lax.all_to_all(rel_local.reshape(BUCKETS, LANES, LANES), "bucket",
                               split_axis=0, concat_axis=0, tiled=True)
    grad = call(
        functools.partial(entity_kernel, 8, negatives), "entities", shape((ROWS, LANES), F32),
        [SM] * 4 + [VM] * 3,
        [pltpu.VMEM((BUCKETS * LANES, LANES), F32)] + [wide] * 4, size=60000000,
    )(head_row, pad, asked.reshape(BUCKETS * LANES), slopes.reshape(BUCKETS * LANES), head_grad,
      neg_grad, came.reshape(BUCKETS * LANES, LANES))
    relation_grad = jnp.sum(rel_parts.astype(F32), axis=0)
    return (loss.reshape(EDGES), grad, relation_grad)


def solution(mesh):
    in_specs = (
        P("bucket", "col"),
        P(None, "col"),
        P("bucket"),
        P("bucket"),
        P("bucket", None),
        P("bucket"),
        P("bucket", None),
    )
    out_specs = (P("bucket"), P("bucket", "col"), P("bucket", "col"))
    return jax.shard_map(body, mesh=mesh, in_specs=in_specs, out_specs=out_specs, check_vma=False)
```

```python
import functools

import jax
import jax.numpy as jnp
from jax import lax
from jax.experimental import pallas as pl
from jax.experimental.pallas import tpu as pltpu
from jax.sharding import PartitionSpec as P

LANES = 128
SPAN = 512
NEG_PAD = 1024
ROWS = 8192
DUMP = 8192
RELS = 4096
EDGES = 2048
BUCKETS = 32
COLS = 8
UNROLL = 64
CHIPS = 4
F32 = jnp.float32
BF16 = jnp.bfloat16
VM = pl.BlockSpec(memory_space=pltpu.VMEM)
SM = pl.BlockSpec(memory_space=pltpu.SMEM)
NT = (((1,), (1,)), ((), ()))
TN = (((0,), (0,)), ((), ()))


def call(kernel, name, outs, ins, scratch=(), flops=1000000, size=4000000, group=None):
    remote = {} if group is None else dict(collective_id=group, has_side_effects=True)
    return pl.pallas_call(
        kernel,
        name=name,
        out_shape=outs,
        in_specs=ins,
        out_specs=jax.tree.map(lambda _: VM, outs),
        scratch_shapes=scratch,
        compiler_params=pltpu.CompilerParams(vmem_limit_bytes=56 << 20, **remote),
        cost_estimate=pl.CostEstimate(flops=flops, bytes_accessed=size, transcendentals=0),
    )


def shape(dims, kind):
    return jax.ShapeDtypeStruct(dims, kind)


def iota(dims, axis):
    return lax.broadcasted_iota(jnp.int32, dims, axis)


def to_column(row):
    size = row.shape[1]
    same = iota((size, size), 0) == iota((size, size), 1)
    return jnp.sum(jnp.where(same, row, 0.0), axis=1, keepdims=True)


def to_row(column):
    size = column.shape[0]
    same = iota((size, size), 0) == iota((size, size), 1)
    return jnp.sum(jnp.where(same, column, 0.0), axis=0, keepdims=True)


def swap_halves(value):
    return pltpu.roll(value, LANES // 2, 1)


def times(left, right):
    lane = iota(left.shape, 1)
    first = lane < LANES // 2
    turned = swap_halves(right)
    real = jnp.where(first, right, turned)
    imag = jnp.where(first, -turned, right)
    return left * real + swap_halves(left) * imag


def times_conj(left, right):
    lane = iota(left.shape, 1)
    first = lane < LANES // 2
    turned = swap_halves(right)
    real = jnp.where(first, right, turned)
    imag = jnp.where(first, turned, -right)
    return left * real + swap_halves(left) * imag


def greet(axis, count):
    me = lax.axis_index(axis)
    barrier = pltpu.get_barrier_semaphore()

    def tell(i, carry):
        peer = lax.rem(me + i, count)
        pl.semaphore_signal(barrier, inc=1, device_id={axis: peer},
                            device_id_type=pl.DeviceIdType.MESH)
        return carry

    lax.fori_loop(1, count, tell, 0)
    pl.semaphore_wait(barrier, count - 1)


def spread(axis, count, src, dst, send_sem, recv_sem):
    me = lax.axis_index(axis)

    def send(i, carry):
        peer = lax.rem(me + i, count)
        pltpu.make_async_remote_copy(
            src_ref=src.at[peer], dst_ref=dst.at[me], send_sem=send_sem, recv_sem=recv_sem,
            device_id={axis: peer}, device_id_type=pl.DeviceIdType.MESH).start()
        return carry

    lax.fori_loop(1, count, send, 0)


def settle(axis, count, src, dst, send_sem, recv_sem):
    me = lax.axis_index(axis)
    rest = pl.ds(0, count - 1)
    pltpu.make_async_remote_copy(
        src_ref=src.at[rest], dst_ref=dst.at[rest], send_sem=send_sem, recv_sem=recv_sem,
        device_id={axis: lax.rem(me + 1, count)}, device_id_type=pl.DeviceIdType.MESH).wait()


def load_table(table_ref, wide_ref, rows):
    wide_ref[0:rows, :] = table_ref[...].astype(F32)


def to(peers):
    return dict(device_id=peers, device_id_type=pl.DeviceIdType.MESH)


def forward_kernel(negatives, head_ref, rel_ref, neg_ref, owner_ref, row_ref, table_ref, rtable_ref,
                   asked_ref, came_ref, slopes_ref, loss_ref, head_grad_ref, rel_grad_ref,
                   neg_grad_ref,
                   wide, rwide, prod_wide, heads, rels, tails, raw, weights, tail_wide,
                   target, request, inverse, found, fetched, slots, pack, got, keep, send, other,
                   parts, stats, slope_out, masses, tilts, asked_s, target_s, inverse_s,
                   local_sem, bucket_send, bucket_recv, pack_send, pack_recv, swap_send, swap_recv,
                   weight_send, weight_recv, near_send, near_recv, part_send, part_recv):
    me = lax.axis_index("bucket")
    place = lax.axis_index("col")
    chip, core = place // 2, lax.rem(place, 2)
    near = {"col": 2 * chip + (1 - core)}

    barrier = pltpu.get_barrier_semaphore()
    for axis, count in (("bucket", BUCKETS), ("col", COLS)):
        def tell(i, carry):
            peer = lax.rem(lax.axis_index(axis) + i, count)
            pl.semaphore_signal(barrier, inc=1, **to({axis: peer}))
            return carry

        lax.fori_loop(1, count, tell, 0)
    lower = (iota((LANES, LANES), 0) <= iota((LANES, LANES), 1)).astype(BF16)
    before = jnp.zeros((BUCKETS, 1), F32)
    high = jnp.zeros((BUCKETS, LANES), F32)
    low = jnp.zeros((BUCKETS, LANES), F32)
    for block in range(EDGES // LANES):
        at = slice(block * LANES, (block + 1) * LANES)
        owner = owner_ref[:, at]
        row = row_ref[:, at]
        mine = iota((BUCKETS, LANES), 0) == owner
        hit = mine.astype(F32).astype(BF16)
        count = jnp.dot(hit, lower, preferred_element_type=F32)
        ranks = jnp.where(mine, count + before - 1.0, 0.0)
        rank = jnp.sum(ranks, axis=0, keepdims=True).astype(jnp.int32)
        before = before + count[:, LANES - 1 : LANES]
        target[block] = jnp.clip(owner * LANES + rank, 0, BUCKETS * LANES - 1)
        slot = iota((LANES, LANES), 0) == rank

        def placed(values):
            spread_out = jnp.where(slot, values, 0.0).astype(BF16)
            return lax.dot_general(hit, spread_out, NT, preferred_element_type=F32)

        high = high + placed((row >> 7).astype(F32))
        low = low + placed((row & 127).astype(F32))
    used = iota((BUCKETS, LANES), 1).astype(F32) < before
    rows = jnp.where(used, high * 128.0 + low, float(DUMP)).astype(jnp.int32)
    for owner in range(BUCKETS):
        request[owner] = jnp.clip(rows[owner : owner + 1, :], 0, DUMP)

    pl.semaphore_wait(barrier, BUCKETS + COLS - 2)
    spread("bucket", BUCKETS, request, asked_ref, bucket_send.at[0], bucket_recv.at[0])
    target_copy = pltpu.make_async_copy(target, target_s, local_sem.at[0])
    target_copy.start()
    asked_ref[me] = request[me]

    load_table(table_ref, wide, ROWS)
    load_table(rtable_ref, rwide, RELS)
    wide[ROWS : ROWS + 8, :] = jnp.zeros((8, LANES), F32)
    prod_wide[EDGES : EDGES + 8, :] = jnp.zeros((8, LANES), F32)

    def pack_copy(step):
        return pltpu.make_async_remote_copy(
            src_ref=pack.at[step], dst_ref=got.at[step], send_sem=pack_send.at[step],
            recv_sem=pack_recv.at[step], **to({"col": 2 * lax.rem(chip + step, CHIPS) + core}))

    def fill(step):
        span = lax.rem(chip + step, CHIPS)

        def edge_step(j, carry):
            base = pl.multiple_of(span * SPAN + j * UNROLL, UNROLL)
            head = jnp.concatenate(
                [wide[pl.ds(head_ref[base + r], 1), :] for r in range(UNROLL)], axis=0)
            rel = jnp.concatenate(
                [rwide[pl.ds(rel_ref[base + r], 1), :] for r in range(UNROLL)], axis=0)
            product = times(head, rel).astype(BF16)
            at = pl.ds(base, UNROLL)
            pack[step, pl.ds(pl.multiple_of(NEG_PAD + j * UNROLL, UNROLL), UNROLL), :] = product
            prod_wide[at, :] = product.astype(F32)
            heads[at, :] = head
            rels[at, :] = rel
            return carry

        lax.fori_loop(0, SPAN // UNROLL, edge_step, 0)

        def neg_step(j, carry):
            base = pl.multiple_of(j * UNROLL, UNROLL)
            start = span * negatives + j * UNROLL
            rows = jnp.concatenate(
                [wide[pl.ds(neg_ref[start + r], 1), :] for r in range(UNROLL)],
                axis=0).astype(BF16)
            pack[step, pl.ds(base, UNROLL), :] = rows
            return carry

        whole = negatives // UNROLL
        lax.fori_loop(0, whole, neg_step, 0)
        rest = negatives - whole * UNROLL
        start = span * negatives + whole * UNROLL
        rows = [wide[pl.ds(neg_ref[start + r], 1), :] for r in range(rest)]
        rows.append(jnp.zeros((NEG_PAD - negatives, LANES), F32))
        pack[step, whole * UNROLL : NEG_PAD, :] = jnp.concatenate(rows, axis=0).astype(BF16)

    fill(2)
    pack_copy(2).start()
    fill(1)
    pack_copy(1).start()
    settle("bucket", BUCKETS, request, asked_ref, bucket_send.at[0], bucket_recv.at[0])
    copy = pltpu.make_async_copy(asked_ref, asked_s, local_sem.at[2])
    copy.start()
    copy.wait()

    def bucket_copy(src, dst, which, peer):
        return pltpu.make_async_remote_copy(
            src_ref=src.at[peer], dst_ref=dst.at[me], send_sem=bucket_send.at[which],
            recv_sem=bucket_recv.at[which], **to({"bucket": peer}))

    def take(source, index, out, s):
        for part in range(LANES // UNROLL):
            rows = jnp.concatenate(
                [source[pl.ds(index[s, 0, part * UNROLL + r], 1), :] for r in range(UNROLL)],
                axis=0)
            out[s, part * UNROLL : (part + 1) * UNROLL, :] = rows.astype(BF16)

    def find(i, carry):
        peer = lax.rem(me + i, BUCKETS)
        take(wide, asked_s, found, peer)
        bucket_copy(found, fetched, 1, peer).start()
        return carry

    lax.fori_loop(1, BUCKETS, find, 0)
    take(wide, asked_s, fetched, me)

    fill(3)
    pack_copy(3).start()

    fill(0)

    lane = iota((LANES, LANES), 1).astype(F32)
    edges = jnp.zeros((BUCKETS, LANES), F32)
    for block in range(EDGES // LANES):
        goal = target[block]
        hit = (iota((BUCKETS, LANES), 0) == (goal >> 7)).astype(F32).astype(BF16)
        slot = iota((LANES, LANES), 0) == (goal & 127)
        one = jnp.where(slot, 1.0, 0.0).astype(BF16)
        inner = jnp.where(slot, lane, 0.0).astype(BF16)
        edges = (edges + lax.dot_general(hit, inner, NT, preferred_element_type=F32)
                 + float(block * LANES) * lax.dot_general(
                     hit, one, NT, preferred_element_type=F32))
    edges = jnp.where(used, edges, float(EDGES)).astype(jnp.int32)
    for owner in range(BUCKETS):
        inverse[owner] = jnp.clip(edges[owner : owner + 1, :], 0, EDGES)
    inverse_copy = pltpu.make_async_copy(inverse, inverse_s, local_sem.at[1])
    inverse_copy.start()
    inverse_copy.wait()
    target_copy.wait()

    def give(i, carry):
        peer = lax.rem(me + i, BUCKETS)
        take(prod_wide, inverse_s, slots, peer)
        bucket_copy(slots, came_ref, 2, peer).start()
        return carry

    lax.fori_loop(1, BUCKETS, give, 0)
    take(prod_wide, inverse_s, came_ref, me)

    for step in range(1, CHIPS):
        pack_copy(step).wait()
    halves = SPAN // 2

    def swap(block):
        at = pl.ds(block * LANES, LANES)
        return pltpu.make_async_remote_copy(
            src_ref=send.at[at], dst_ref=other.at[at], send_sem=swap_send.at[block],
            recv_sem=swap_recv.at[block], **to(near))

    def score(half, out, block):
        at = pl.ds(pl.multiple_of(NEG_PAD + half * halves + block * LANES, LANES), LANES)
        parts_of = [pack.at[0]] + [got.at[step] for step in range(1, CHIPS)]
        left = jnp.concatenate([q[at, :] for q in parts_of], axis=1)

        def piece(i, carry):
            cut = pl.ds(pl.multiple_of(i * 256, 256), 256)
            right = jnp.concatenate([q[cut, :] for q in parts_of], axis=1)
            out[block * LANES : (block + 1) * LANES, cut] = lax.dot_general(
                left, right, NT, preferred_element_type=F32)
            return carry

        lax.fori_loop(0, NEG_PAD // 256, piece, 0)

    def source(step, side):
        return 2 * lax.rem(chip - step + CHIPS, CHIPS) + side

    def weight_copy(step, block, piece):
        ref = weights.at[piece, pl.ds(block * LANES, LANES)]
        flag = step * 2 + block
        return pltpu.make_async_remote_copy(
            src_ref=ref, dst_ref=ref, send_sem=weight_send.at[flag],
            recv_sem=weight_recv.at[flag],
            **to({"col": 2 * lax.rem(chip + step, CHIPS) + core}))

    def near_copy(step, block, side):
        ref = weights.at[source(step, side), pl.ds(block * LANES, LANES)]
        flag = step * 2 + block
        return pltpu.make_async_remote_copy(
            src_ref=ref, dst_ref=ref, send_sem=near_send.at[flag], recv_sem=near_recv.at[flag],
            **to(near))

    def blend(step, block, side):
        piece = source(step, side)
        at = pl.ds(pl.multiple_of(piece * halves + block * LANES, LANES), LANES)
        raw[at, :] = jnp.dot(weights[piece, block * LANES : (block + 1) * LANES, :],
                             pack[(CHIPS - step) % CHIPS, 0:NEG_PAD, :],
                             preferred_element_type=F32)

    def publish(block):
        for step in (2, 1, 3):
            weight_copy(step, block, place).start()
        near_copy(0, block, core).start()

    def finish(step, block, side):
        blend(step, block, side)
        piece = source(step, side)
        span = piece // 2
        at = pl.ds(pl.multiple_of(piece * halves + block * LANES, LANES), LANES)
        scale = to_column(masses[piece * 2 + block])
        scaled = (prod_wide[at, :] * scale).astype(BF16)
        down = raw[at, :] * scale + to_column(tilts[piece * 2 + block]) * tails[at, :]
        head_grad_ref[at, :] = times_conj(down, rels[at, :])
        rel_grad_ref[at, :] = times_conj(down, heads[at, :])
        neg_grad_ref[span] = neg_grad_ref[span] + lax.dot_general(
            weights[piece, block * LANES : (block + 1) * LANES, :], scaled, TN,
            preferred_element_type=F32)

    for block in range(2):
        score(1 - core, send, block)
        swap(block).start()
    for block in range(2):
        score(core, keep, block)
    for block in range(2):
        swap(block).wait()
        at = slice(block * LANES, (block + 1) * LANES)
        scores = keep[at, :] + other[at, :]
        real = iota((LANES, NEG_PAD), 1) < negatives
        scores = jnp.where(real, scores, -jnp.inf)
        top = jnp.max(scores, axis=1, keepdims=True)
        expo = jnp.exp(scores - top)
        weights[place, at, :] = expo.astype(BF16)
        if block == 0:
            publish(block)
        stats[place, 0:1, at] = to_row(top)
        stats[place, 1:2, at] = to_row(jnp.sum(expo, axis=1, keepdims=True))

    settle("bucket", BUCKETS, found, fetched, bucket_send.at[1], bucket_recv.at[1])
    tail_wide[...] = fetched[...].reshape(BUCKETS * LANES, LANES).astype(F32)

    def tail_step(block, carry):
        base = pl.multiple_of(block * LANES, LANES)
        for part in range(LANES // UNROLL):
            rows = jnp.concatenate(
                [tail_wide[pl.ds(target_s[block, 0, part * UNROLL + r], 1), :]
                 for r in range(UNROLL)], axis=0)
            tails[pl.ds(pl.multiple_of(base + part * UNROLL, UNROLL), UNROLL), :] = rows
        at = pl.ds(base, LANES)
        both = tails[at, :] * prod_wide[at, :]
        parts[place, block] = to_row(jnp.sum(both, axis=1, keepdims=True))
        return carry

    lax.fori_loop(0, EDGES // LANES, tail_step, 0)

    def part_copy(k, ref, peer):
        return pltpu.make_async_remote_copy(
            src_ref=ref.at[place], dst_ref=ref.at[place], send_sem=part_send.at[k],
            recv_sem=part_recv.at[k], **to({"col": peer}))

    def tell_parts(i, carry):
        peer = lax.rem(place + i, COLS)
        part_copy(0, parts, peer).start()
        part_copy(1, stats, peer).start()
        return carry

    lax.fori_loop(1, COLS, tell_parts, 0)

    publish(1)
    neg_grad_ref[...] = jnp.zeros_like(neg_grad_ref)
    for step in (1, 3, 2):
        weight_copy(step, 0, source(step, core)).wait_recv()
        near_copy(step, 0, core).start()
    rest = pl.ds(0, COLS - 1)
    for k, ref in enumerate((parts, stats)):
        pltpu.make_async_remote_copy(
            src_ref=ref.at[rest], dst_ref=ref.at[rest], send_sem=part_send.at[k],
            recv_sem=part_recv.at[k], **to(near)).wait()

    deal = jnp.zeros((BUCKETS, LANES), F32)
    for block in range(EDGES // LANES):
        part, inner = block // 2, (block % 2) * LANES
        high = stats[part, 0:1, inner : inner + LANES]
        mass = stats[part, 1:2, inner : inner + LANES]
        positive = parts[0, block]
        for k in range(1, COLS):
            positive = positive + parts[k, block]
        top = jnp.maximum(high, positive)
        shrink = jnp.exp(high - top)
        expo = jnp.exp(positive - top)
        total = mass * shrink + expo
        slope = expo / total - 1.0
        loss_ref[block] = top + jnp.log(total) - positive
        masses[block] = shrink / total
        tilts[block] = slope
        goal = target[block]
        hit = (iota((BUCKETS, LANES), 0) == (goal >> 7)).astype(F32).astype(BF16)
        slot = iota((LANES, LANES), 0) == (goal & 127)
        left_over = slope
        for _ in range(3):
            piece = left_over.astype(BF16)
            spread_out = jnp.where(slot, piece.astype(F32), 0.0).astype(BF16)
            deal = deal + lax.dot_general(hit, spread_out, NT, preferred_element_type=F32)
            left_over = left_over - piece.astype(F32)
    for owner in range(BUCKETS):
        slope_out[owner] = deal[owner : owner + 1, :]
    spread("bucket", BUCKETS, slope_out, slopes_ref, bucket_send.at[3], bucket_recv.at[3])
    slopes_ref[me] = slope_out[me]

    finish(0, 0, core)
    finish(0, 1, core)
    for block in range(2):
        near_copy(0, block, 1 - core).wait_recv()
        finish(0, block, 1 - core)
    for step in (1, 3, 2):
        finish(step, 0, core)
    for step in (1, 3, 2):
        near_copy(step, 0, 1 - core).wait_recv()
        finish(step, 0, 1 - core)
    for step in (1, 3, 2):
        weight_copy(step, 1, source(step, core)).wait_recv()
        near_copy(step, 1, core).start()
        finish(step, 1, core)
    for step in (1, 3, 2):
        near_copy(step, 1, 1 - core).wait_recv()
        finish(step, 1, 1 - core)
    for block in range(2):
        for step in range(CHIPS):
            near_copy(step, block, core).wait_send()
        for step in range(1, CHIPS):
            weight_copy(step, block, place).wait_send()
    settle("bucket", BUCKETS, slope_out, slopes_ref, bucket_send.at[3], bucket_recv.at[3])
    settle("bucket", BUCKETS, slots, came_ref, bucket_send.at[2], bucket_recv.at[2])

def relation_kernel(unroll, rel_ref, grad_ref, out_ref, a0, a1, a2, a3):
    sums = (a0, a1, a2, a3)
    for one in sums:
        one[...] = jnp.zeros_like(one)

    def step(j, carry):
        for r in range(unroll):
            for k, one in enumerate(sums):
                edge = k * SPAN + j * unroll + r
                place = pl.ds(rel_ref[edge], 1)
                one[place, :] = one[place, :] + grad_ref[pl.ds(edge, 1), :]
        return carry

    lax.fori_loop(0, SPAN // unroll, step, 0)
    out_ref[...] = ((a0[...] + a1[...]) + (a2[...] + a3[...])).astype(BF16)


def entity_kernel(unroll, negatives, head_ref, neg_ref, asked_ref, slope_ref, head_grad_ref,
                  neg_grad_ref, came_ref, out_ref, wide, a0, a1, a2, a3):
    sums = (a0, a1, a2, a3)
    for one in sums:
        one[...] = jnp.zeros_like(one)
    wide[...] = came_ref[...].astype(F32)

    def edge_step(j, carry):
        for r in range(unroll):
            for k, one in enumerate(sums):
                edge = k * SPAN + j * unroll + r
                place = pl.ds(head_ref[edge], 1)
                one[place, :] = one[place, :] + head_grad_ref[pl.ds(edge, 1), :]
        return carry

    lax.fori_loop(0, SPAN // unroll, edge_step, 0)

    def neg_step(j, carry):
        for r in range(unroll):
            for k, one in enumerate(sums):
                place = pl.ds(neg_ref[k * negatives + j * unroll + r], 1)
                one[place, :] = one[place, :] + neg_grad_ref[k, pl.ds(j * unroll + r, 1), :]
        return carry

    lax.fori_loop(0, negatives // unroll, neg_step, 0)
    each = BUCKETS // 4

    def source(s, carry):
        def group(j):
            for r in range(unroll):
                for k, one in enumerate(sums):
                    owner = k * each + s
                    slot = j * unroll + r
                    place = pl.ds(asked_ref[owner * LANES + slot], 1)
                    term = slope_ref[owner * LANES + slot] * wide[pl.ds(owner * LANES + slot, 1), :]
                    one[place, :] = one[place, :] + term
            return j + 1

        def more(j):
            at = jnp.minimum(j * unroll, LANES - 1)
            first = asked_ref[s * LANES + at]
            for k in range(1, 4):
                first = jnp.minimum(first, asked_ref[(k * each + s) * LANES + at])
            return jnp.logical_and(j * unroll < LANES, first < DUMP)

        lax.while_loop(more, group, 0)
        return carry

    lax.fori_loop(0, each, source, 0)
    total = (a0[0:ROWS, :] + a1[0:ROWS, :]) + (a2[0:ROWS, :] + a3[0:ROWS, :])
    out_ref[...] = total


def body(entity_table, relation_table, head_row, relation_id, tail_owner, tail_row, negative_row):
    negatives = negative_row.shape[1]
    negs = negative_row.reshape(CHIPS * negatives)
    wide = pltpu.VMEM((ROWS + 8, LANES), F32)
    lists = (BUCKETS, 1, LANES)
    blocks = (EDGES // LANES, 1, LANES)
    grid = (BUCKETS, LANES, LANES)
    half = pltpu.VMEM((SPAN // 2, NEG_PAD), F32)
    packs = pltpu.VMEM((CHIPS, NEG_PAD + SPAN, LANES), BF16)
    flag = pltpu.SemaphoreType.DMA
    flat32 = pltpu.VMEM((EDGES, LANES), F32)
    asked, came, slopes, loss, head_grad, rel_grad, neg_grad = call(
        functools.partial(forward_kernel, negatives), "forward",
        (shape(lists, jnp.int32), shape(grid, BF16), shape(lists, F32), shape(blocks, F32),
         shape((EDGES, LANES), F32), shape((EDGES, LANES), F32),
         shape((CHIPS, NEG_PAD, LANES), F32)),
        [SM] * 3 + [VM] * 4,
        [wide, pltpu.VMEM((RELS, LANES), F32), pltpu.VMEM((EDGES + 8, LANES), F32),
         flat32, flat32, flat32, flat32,
         pltpu.VMEM((COLS, SPAN // 2, NEG_PAD), BF16),
         pltpu.VMEM((BUCKETS * LANES, LANES), F32), pltpu.VMEM(blocks, jnp.int32),
         pltpu.VMEM(lists, jnp.int32), pltpu.VMEM(lists, jnp.int32),
         pltpu.VMEM(grid, BF16), pltpu.VMEM(grid, BF16), pltpu.VMEM(grid, BF16),
         packs, packs, half, half, half,
         pltpu.VMEM((COLS,) + blocks, F32), pltpu.VMEM((COLS, 2, SPAN // 2), F32),
         pltpu.VMEM(lists, F32), pltpu.VMEM(blocks, F32), pltpu.VMEM(blocks, F32),
         pltpu.SMEM(lists, jnp.int32),
         pltpu.SMEM(blocks, jnp.int32), pltpu.SMEM(lists, jnp.int32),
         flag((3,)), flag((4,)), flag((4,)), flag((CHIPS,)), flag((CHIPS,)), flag((2,)),
         flag((2,)), flag((2 * CHIPS,)), flag((2 * CHIPS,)), flag((2 * CHIPS,)),
         flag((2 * CHIPS,)), flag((2,)), flag((2,))],
        flops=600000000, size=40000000, group=0,
    )(head_row, relation_id, negs, tail_owner.reshape(1, EDGES), tail_row.reshape(1, EDGES),
      entity_table, relation_table)

    rel_local = call(
        functools.partial(relation_kernel, 8), "relations", shape((RELS, LANES), BF16),
        [SM, VM], [pltpu.VMEM((RELS, LANES), F32)] * 4, size=10000000,
    )(relation_id, rel_grad)
    rel_parts = lax.all_to_all(rel_local.reshape(BUCKETS, LANES, LANES), "bucket",
                               split_axis=0, concat_axis=0, tiled=True)
    grad = call(
        functools.partial(entity_kernel, 8, negatives), "entities", shape((ROWS, LANES), F32),
        [SM] * 4 + [VM] * 3,
        [pltpu.VMEM((BUCKETS * LANES, LANES), F32)] + [wide] * 4, size=60000000,
    )(head_row, negs, asked.reshape(BUCKETS * LANES), slopes.reshape(BUCKETS * LANES), head_grad,
      neg_grad, came.reshape(BUCKETS * LANES, LANES))
    relation_grad = jnp.sum(rel_parts.astype(F32), axis=0)
    return (loss.reshape(EDGES), grad, relation_grad)


def solution(mesh):
    in_specs = (
        P("bucket", "col"),
        P(None, "col"),
        P("bucket"),
        P("bucket"),
        P("bucket", None),
        P("bucket"),
        P("bucket", None),
    )
    out_specs = (P("bucket"), P("bucket", "col"), P("bucket", "col"))
    return jax.shard_map(body, mesh=mesh, in_specs=in_specs, out_specs=out_specs, check_vma=False)
```

```python
import functools

import jax
import jax.numpy as jnp
from jax import lax
from jax.experimental import pallas as pl
from jax.experimental.pallas import tpu as pltpu
from jax.sharding import PartitionSpec as P

LANES = 128
SPAN = 512
NEG_PAD = 1024
ROWS = 8192
DUMP = 8192
RELS = 4096
EDGES = 2048
BUCKETS = 32
COLS = 8
UNROLL = 128
CHIPS = 4
F32 = jnp.float32
BF16 = jnp.bfloat16
VM = pl.BlockSpec(memory_space=pltpu.VMEM)
SM = pl.BlockSpec(memory_space=pltpu.SMEM)
NT = (((1,), (1,)), ((), ()))
TN = (((0,), (0,)), ((), ()))


def call(kernel, name, outs, ins, scratch=(), flops=1000000, size=4000000, group=None):
    remote = {} if group is None else dict(collective_id=group, has_side_effects=True)
    return pl.pallas_call(
        kernel,
        name=name,
        out_shape=outs,
        in_specs=ins,
        out_specs=jax.tree.map(lambda _: VM, outs),
        scratch_shapes=scratch,
        compiler_params=pltpu.CompilerParams(vmem_limit_bytes=56 << 20, **remote),
        cost_estimate=pl.CostEstimate(flops=flops, bytes_accessed=size, transcendentals=0),
    )


def shape(dims, kind):
    return jax.ShapeDtypeStruct(dims, kind)


def iota(dims, axis):
    return lax.broadcasted_iota(jnp.int32, dims, axis)


def to_column(row):
    size = row.shape[1]
    same = iota((size, size), 0) == iota((size, size), 1)
    return jnp.sum(jnp.where(same, row, 0.0), axis=1, keepdims=True)


def to_row(column):
    size = column.shape[0]
    same = iota((size, size), 0) == iota((size, size), 1)
    return jnp.sum(jnp.where(same, column, 0.0), axis=0, keepdims=True)


def swap_halves(value):
    return pltpu.roll(value, LANES // 2, 1)


def times(left, right):
    lane = iota(left.shape, 1)
    first = lane < LANES // 2
    turned = swap_halves(right)
    real = jnp.where(first, right, turned)
    imag = jnp.where(first, -turned, right)
    return left * real + swap_halves(left) * imag


def times_conj(left, right):
    lane = iota(left.shape, 1)
    first = lane < LANES // 2
    turned = swap_halves(right)
    real = jnp.where(first, right, turned)
    imag = jnp.where(first, turned, -right)
    return left * real + swap_halves(left) * imag


def greet(axis, count):
    me = lax.axis_index(axis)
    barrier = pltpu.get_barrier_semaphore()

    def tell(i, carry):
        peer = lax.rem(me + i, count)
        pl.semaphore_signal(barrier, inc=1, device_id={axis: peer},
                            device_id_type=pl.DeviceIdType.MESH)
        return carry

    lax.fori_loop(1, count, tell, 0)
    pl.semaphore_wait(barrier, count - 1)


def spread(axis, count, src, dst, send_sem, recv_sem):
    me = lax.axis_index(axis)

    def send(i, carry):
        peer = lax.rem(me + i, count)
        pltpu.make_async_remote_copy(
            src_ref=src.at[peer], dst_ref=dst.at[me], send_sem=send_sem, recv_sem=recv_sem,
            device_id={axis: peer}, device_id_type=pl.DeviceIdType.MESH).start()
        return carry

    lax.fori_loop(1, count, send, 0)


def settle(axis, count, src, dst, send_sem, recv_sem):
    me = lax.axis_index(axis)
    rest = pl.ds(0, count - 1)
    pltpu.make_async_remote_copy(
        src_ref=src.at[rest], dst_ref=dst.at[rest], send_sem=send_sem, recv_sem=recv_sem,
        device_id={axis: lax.rem(me + 1, count)}, device_id_type=pl.DeviceIdType.MESH).wait()


def load_table(table_ref, wide_ref, rows):
    wide_ref[0:rows, :] = table_ref[...].astype(F32)


def to(peers):
    return dict(device_id=peers, device_id_type=pl.DeviceIdType.MESH)


def forward_kernel(negatives, head_ref, rel_ref, neg_ref, owner_ref, row_ref, table_ref, rtable_ref,
                   asked_ref, came_ref, slopes_ref, loss_ref, head_grad_ref, rel_grad_ref,
                   neg_grad_ref,
                   wide, rwide, prod_wide, heads, rels, tails, raw, weights, tail_wide,
                   target, request, inverse, found, fetched, slots, pack, got, keep, send, other,
                   parts, stats, slope_out, masses, tilts, asked_s, target_s, inverse_s,
                   local_sem, bucket_send, bucket_recv, pack_send, pack_recv, swap_send, swap_recv,
                   weight_send, weight_recv, near_send, near_recv, part_send, part_recv):
    me = lax.axis_index("bucket")
    place = lax.axis_index("col")
    chip, core = place // 2, lax.rem(place, 2)
    near = {"col": 2 * chip + (1 - core)}

    barrier = pltpu.get_barrier_semaphore()
    for axis, count in (("bucket", BUCKETS), ("col", COLS)):
        def tell(i, carry):
            peer = lax.rem(lax.axis_index(axis) + i, count)
            pl.semaphore_signal(barrier, inc=1, **to({axis: peer}))
            return carry

        lax.fori_loop(1, count, tell, 0)
    lower = (iota((LANES, LANES), 0) <= iota((LANES, LANES), 1)).astype(BF16)
    before = jnp.zeros((BUCKETS, 1), F32)
    high = jnp.zeros((BUCKETS, LANES), F32)
    low = jnp.zeros((BUCKETS, LANES), F32)
    for block in range(EDGES // LANES):
        at = slice(block * LANES, (block + 1) * LANES)
        owner = owner_ref[:, at]
        row = row_ref[:, at]
        mine = iota((BUCKETS, LANES), 0) == owner
        hit = mine.astype(F32).astype(BF16)
        count = jnp.dot(hit, lower, preferred_element_type=F32)
        ranks = jnp.where(mine, count + before - 1.0, 0.0)
        rank = jnp.sum(ranks, axis=0, keepdims=True).astype(jnp.int32)
        before = before + count[:, LANES - 1 : LANES]
        target[block] = jnp.clip(owner * LANES + rank, 0, BUCKETS * LANES - 1)
        slot = iota((LANES, LANES), 0) == rank

        def placed(values):
            spread_out = jnp.where(slot, values, 0.0).astype(BF16)
            return lax.dot_general(hit, spread_out, NT, preferred_element_type=F32)

        high = high + placed((row >> 7).astype(F32))
        low = low + placed((row & 127).astype(F32))
    used = iota((BUCKETS, LANES), 1).astype(F32) < before
    rows = jnp.where(used, high * 128.0 + low, float(DUMP)).astype(jnp.int32)
    for owner in range(BUCKETS):
        request[owner] = jnp.clip(rows[owner : owner + 1, :], 0, DUMP)

    pl.semaphore_wait(barrier, BUCKETS + COLS - 2)
    spread("bucket", BUCKETS, request, asked_ref, bucket_send.at[0], bucket_recv.at[0])
    target_copy = pltpu.make_async_copy(target, target_s, local_sem.at[0])
    target_copy.start()
    asked_ref[me] = request[me]

    load_table(table_ref, wide, ROWS)
    load_table(rtable_ref, rwide, RELS)
    wide[ROWS : ROWS + 8, :] = jnp.zeros((8, LANES), F32)
    prod_wide[EDGES : EDGES + 8, :] = jnp.zeros((8, LANES), F32)

    def pack_copy(step):
        return pltpu.make_async_remote_copy(
            src_ref=pack.at[step], dst_ref=got.at[step], send_sem=pack_send.at[step],
            recv_sem=pack_recv.at[step], **to({"col": 2 * lax.rem(chip + step, CHIPS) + core}))

    def fill(step):
        span = lax.rem(chip + step, CHIPS)

        def edge_step(j, carry):
            base = pl.multiple_of(span * SPAN + j * UNROLL, UNROLL)
            head = jnp.concatenate(
                [wide[pl.ds(head_ref[base + r], 1), :] for r in range(UNROLL)], axis=0)
            rel = jnp.concatenate(
                [rwide[pl.ds(rel_ref[base + r], 1), :] for r in range(UNROLL)], axis=0)
            product = times(head, rel).astype(BF16)
            at = pl.ds(base, UNROLL)
            pack[step, pl.ds(pl.multiple_of(NEG_PAD + j * UNROLL, UNROLL), UNROLL), :] = product
            prod_wide[at, :] = product.astype(F32)
            heads[at, :] = head
            rels[at, :] = rel
            return carry

        lax.fori_loop(0, SPAN // UNROLL, edge_step, 0)

        def neg_step(j, carry):
            base = pl.multiple_of(j * UNROLL, UNROLL)
            start = span * negatives + j * UNROLL
            rows = jnp.concatenate(
                [wide[pl.ds(neg_ref[start + r], 1), :] for r in range(UNROLL)],
                axis=0).astype(BF16)
            pack[step, pl.ds(base, UNROLL), :] = rows
            return carry

        whole = negatives // UNROLL
        lax.fori_loop(0, whole, neg_step, 0)
        rest = negatives - whole * UNROLL
        start = span * negatives + whole * UNROLL
        rows = [wide[pl.ds(neg_ref[start + r], 1), :] for r in range(rest)]
        rows.append(jnp.zeros((NEG_PAD - negatives, LANES), F32))
        pack[step, whole * UNROLL : NEG_PAD, :] = jnp.concatenate(rows, axis=0).astype(BF16)

    fill(2)
    pack_copy(2).start()
    fill(1)
    pack_copy(1).start()
    settle("bucket", BUCKETS, request, asked_ref, bucket_send.at[0], bucket_recv.at[0])
    copy = pltpu.make_async_copy(asked_ref, asked_s, local_sem.at[2])
    copy.start()
    copy.wait()

    def bucket_copy(src, dst, which, peer):
        return pltpu.make_async_remote_copy(
            src_ref=src.at[peer], dst_ref=dst.at[me], send_sem=bucket_send.at[which],
            recv_sem=bucket_recv.at[which], **to({"bucket": peer}))

    def take(source, index, out, s):
        for part in range(LANES // UNROLL):
            rows = jnp.concatenate(
                [source[pl.ds(index[s, 0, part * UNROLL + r], 1), :] for r in range(UNROLL)],
                axis=0)
            out[s, part * UNROLL : (part + 1) * UNROLL, :] = rows.astype(BF16)

    def find(i, carry):
        peer = lax.rem(me + i, BUCKETS)
        take(wide, asked_s, found, peer)
        bucket_copy(found, fetched, 1, peer).start()
        return carry

    lax.fori_loop(1, BUCKETS, find, 0)
    take(wide, asked_s, fetched, me)

    fill(3)
    pack_copy(3).start()

    fill(0)

    lane = iota((LANES, LANES), 1).astype(F32)
    edges = jnp.zeros((BUCKETS, LANES), F32)
    for block in range(EDGES // LANES):
        goal = target[block]
        hit = (iota((BUCKETS, LANES), 0) == (goal >> 7)).astype(F32).astype(BF16)
        slot = iota((LANES, LANES), 0) == (goal & 127)
        one = jnp.where(slot, 1.0, 0.0).astype(BF16)
        inner = jnp.where(slot, lane, 0.0).astype(BF16)
        edges = (edges + lax.dot_general(hit, inner, NT, preferred_element_type=F32)
                 + float(block * LANES) * lax.dot_general(
                     hit, one, NT, preferred_element_type=F32))
    edges = jnp.where(used, edges, float(EDGES)).astype(jnp.int32)
    for owner in range(BUCKETS):
        inverse[owner] = jnp.clip(edges[owner : owner + 1, :], 0, EDGES)
    inverse_copy = pltpu.make_async_copy(inverse, inverse_s, local_sem.at[1])
    inverse_copy.start()
    inverse_copy.wait()
    target_copy.wait()

    def give(i, carry):
        peer = lax.rem(me + i, BUCKETS)
        take(prod_wide, inverse_s, slots, peer)
        bucket_copy(slots, came_ref, 2, peer).start()
        return carry

    lax.fori_loop(1, BUCKETS, give, 0)
    take(prod_wide, inverse_s, came_ref, me)

    for step in range(1, CHIPS):
        pack_copy(step).wait()
    halves = SPAN // 2

    def swap(block):
        at = pl.ds(block * LANES, LANES)
        return pltpu.make_async_remote_copy(
            src_ref=send.at[at], dst_ref=other.at[at], send_sem=swap_send.at[block],
            recv_sem=swap_recv.at[block], **to(near))

    def score(half, out, block):
        at = pl.ds(pl.multiple_of(NEG_PAD + half * halves + block * LANES, LANES), LANES)
        parts_of = [pack.at[0]] + [got.at[step] for step in range(1, CHIPS)]
        left = jnp.concatenate([q[at, :] for q in parts_of], axis=1)

        def piece(i, carry):
            cut = pl.ds(pl.multiple_of(i * 256, 256), 256)
            right = jnp.concatenate([q[cut, :] for q in parts_of], axis=1)
            out[block * LANES : (block + 1) * LANES, cut] = lax.dot_general(
                left, right, NT, preferred_element_type=F32)
            return carry

        lax.fori_loop(0, NEG_PAD // 256, piece, 0)

    def source(step, side):
        return 2 * lax.rem(chip - step + CHIPS, CHIPS) + side

    def weight_copy(step, block, piece):
        ref = weights.at[piece, pl.ds(block * LANES, LANES)]
        flag = step * 2 + block
        return pltpu.make_async_remote_copy(
            src_ref=ref, dst_ref=ref, send_sem=weight_send.at[flag],
            recv_sem=weight_recv.at[flag],
            **to({"col": 2 * lax.rem(chip + step, CHIPS) + core}))

    def near_copy(step, block, side):
        ref = weights.at[source(step, side), pl.ds(block * LANES, LANES)]
        flag = step * 2 + block
        return pltpu.make_async_remote_copy(
            src_ref=ref, dst_ref=ref, send_sem=near_send.at[flag], recv_sem=near_recv.at[flag],
            **to(near))

    def blend(step, block, side):
        piece = source(step, side)
        at = pl.ds(pl.multiple_of(piece * halves + block * LANES, LANES), LANES)
        raw[at, :] = jnp.dot(weights[piece, block * LANES : (block + 1) * LANES, :],
                             pack[(CHIPS - step) % CHIPS, 0:NEG_PAD, :],
                             preferred_element_type=F32)

    def publish(block):
        for step in (2, 1, 3):
            weight_copy(step, block, place).start()
        near_copy(0, block, core).start()

    def finish(step, block, side):
        blend(step, block, side)
        piece = source(step, side)
        span = piece // 2
        at = pl.ds(pl.multiple_of(piece * halves + block * LANES, LANES), LANES)
        scale = to_column(masses[piece * 2 + block])
        scaled = (prod_wide[at, :] * scale).astype(BF16)
        down = raw[at, :] * scale + to_column(tilts[piece * 2 + block]) * tails[at, :]
        head_grad_ref[at, :] = times_conj(down, rels[at, :])
        rel_grad_ref[at, :] = times_conj(down, heads[at, :])
        neg_grad_ref[span] = neg_grad_ref[span] + lax.dot_general(
            weights[piece, block * LANES : (block + 1) * LANES, :], scaled, TN,
            preferred_element_type=F32)

    for block in range(2):
        score(1 - core, send, block)
        swap(block).start()
    for block in range(2):
        score(core, keep, block)
    for block in range(2):
        swap(block).wait()
        at = slice(block * LANES, (block + 1) * LANES)
        scores = keep[at, :] + other[at, :]
        real = iota((LANES, NEG_PAD), 1) < negatives
        scores = jnp.where(real, scores, -jnp.inf)
        top = jnp.max(scores, axis=1, keepdims=True)
        expo = jnp.exp(scores - top)
        weights[place, at, :] = expo.astype(BF16)
        if block == 0:
            publish(block)
        stats[place, 0:1, at] = to_row(top)
        stats[place, 1:2, at] = to_row(jnp.sum(expo, axis=1, keepdims=True))

    settle("bucket", BUCKETS, found, fetched, bucket_send.at[1], bucket_recv.at[1])
    tail_wide[...] = fetched[...].reshape(BUCKETS * LANES, LANES).astype(F32)

    def tail_step(block, carry):
        base = pl.multiple_of(block * LANES, LANES)
        for part in range(LANES // UNROLL):
            rows = jnp.concatenate(
                [tail_wide[pl.ds(target_s[block, 0, part * UNROLL + r], 1), :]
                 for r in range(UNROLL)], axis=0)
            tails[pl.ds(pl.multiple_of(base + part * UNROLL, UNROLL), UNROLL), :] = rows
        at = pl.ds(base, LANES)
        both = tails[at, :] * prod_wide[at, :]
        parts[place, block] = to_row(jnp.sum(both, axis=1, keepdims=True))
        return carry

    lax.fori_loop(0, EDGES // LANES, tail_step, 0)

    def part_copy(k, ref, peer):
        return pltpu.make_async_remote_copy(
            src_ref=ref.at[place], dst_ref=ref.at[place], send_sem=part_send.at[k],
            recv_sem=part_recv.at[k], **to({"col": peer}))

    def tell_parts(i, carry):
        peer = lax.rem(place + i, COLS)
        part_copy(0, parts, peer).start()
        part_copy(1, stats, peer).start()
        return carry

    lax.fori_loop(1, COLS, tell_parts, 0)

    publish(1)
    neg_grad_ref[...] = jnp.zeros_like(neg_grad_ref)
    for step in (1, 3, 2):
        weight_copy(step, 0, source(step, core)).wait_recv()
        near_copy(step, 0, core).start()
    rest = pl.ds(0, COLS - 1)
    for k, ref in enumerate((parts, stats)):
        pltpu.make_async_remote_copy(
            src_ref=ref.at[rest], dst_ref=ref.at[rest], send_sem=part_send.at[k],
            recv_sem=part_recv.at[k], **to(near)).wait()

    deal = jnp.zeros((BUCKETS, LANES), F32)
    for block in range(EDGES // LANES):
        part, inner = block // 2, (block % 2) * LANES
        high = stats[part, 0:1, inner : inner + LANES]
        mass = stats[part, 1:2, inner : inner + LANES]
        positive = parts[0, block]
        for k in range(1, COLS):
            positive = positive + parts[k, block]
        top = jnp.maximum(high, positive)
        shrink = jnp.exp(high - top)
        expo = jnp.exp(positive - top)
        total = mass * shrink + expo
        slope = expo / total - 1.0
        loss_ref[block] = top + jnp.log(total) - positive
        masses[block] = shrink / total
        tilts[block] = slope
        goal = target[block]
        hit = (iota((BUCKETS, LANES), 0) == (goal >> 7)).astype(F32).astype(BF16)
        slot = iota((LANES, LANES), 0) == (goal & 127)
        left_over = slope
        for _ in range(3):
            piece = left_over.astype(BF16)
            spread_out = jnp.where(slot, piece.astype(F32), 0.0).astype(BF16)
            deal = deal + lax.dot_general(hit, spread_out, NT, preferred_element_type=F32)
            left_over = left_over - piece.astype(F32)
    for owner in range(BUCKETS):
        slope_out[owner] = deal[owner : owner + 1, :]
    spread("bucket", BUCKETS, slope_out, slopes_ref, bucket_send.at[3], bucket_recv.at[3])
    slopes_ref[me] = slope_out[me]

    finish(0, 0, core)
    finish(0, 1, core)
    for block in range(2):
        near_copy(0, block, 1 - core).wait_recv()
        finish(0, block, 1 - core)
    for step in (1, 3, 2):
        finish(step, 0, core)
    for step in (1, 3, 2):
        near_copy(step, 0, 1 - core).wait_recv()
        finish(step, 0, 1 - core)
    for step in (1, 3, 2):
        weight_copy(step, 1, source(step, core)).wait_recv()
        near_copy(step, 1, core).start()
        finish(step, 1, core)
    for step in (1, 3, 2):
        near_copy(step, 1, 1 - core).wait_recv()
        finish(step, 1, 1 - core)
    for block in range(2):
        for step in range(CHIPS):
            near_copy(step, block, core).wait_send()
        for step in range(1, CHIPS):
            weight_copy(step, block, place).wait_send()
    settle("bucket", BUCKETS, slope_out, slopes_ref, bucket_send.at[3], bucket_recv.at[3])
    settle("bucket", BUCKETS, slots, came_ref, bucket_send.at[2], bucket_recv.at[2])

def relation_kernel(unroll, rel_ref, grad_ref, out_ref, a0, a1, a2, a3):
    sums = (a0, a1, a2, a3)
    for one in sums:
        one[...] = jnp.zeros_like(one)

    def step(j, carry):
        for r in range(unroll):
            for k, one in enumerate(sums):
                edge = k * SPAN + j * unroll + r
                place = pl.ds(rel_ref[edge], 1)
                one[place, :] = one[place, :] + grad_ref[pl.ds(edge, 1), :]
        return carry

    lax.fori_loop(0, SPAN // unroll, step, 0)
    out_ref[...] = ((a0[...] + a1[...]) + (a2[...] + a3[...])).astype(BF16)


def entity_kernel(unroll, negatives, head_ref, neg_ref, asked_ref, slope_ref, head_grad_ref,
                  neg_grad_ref, came_ref, out_ref, wide, a0, a1, a2, a3):
    sums = (a0, a1, a2, a3)
    for one in sums:
        one[...] = jnp.zeros_like(one)
    wide[...] = came_ref[...].astype(F32)

    def edge_step(j, carry):
        for r in range(unroll):
            for k, one in enumerate(sums):
                edge = k * SPAN + j * unroll + r
                place = pl.ds(head_ref[edge], 1)
                one[place, :] = one[place, :] + head_grad_ref[pl.ds(edge, 1), :]
        return carry

    lax.fori_loop(0, SPAN // unroll, edge_step, 0)

    def neg_step(j, carry):
        for r in range(unroll):
            for k, one in enumerate(sums):
                place = pl.ds(neg_ref[k * negatives + j * unroll + r], 1)
                one[place, :] = one[place, :] + neg_grad_ref[k, pl.ds(j * unroll + r, 1), :]
        return carry

    lax.fori_loop(0, negatives // unroll, neg_step, 0)
    each = BUCKETS // 4

    def source(s, carry):
        def group(j):
            for r in range(unroll):
                for k, one in enumerate(sums):
                    owner = k * each + s
                    slot = j * unroll + r
                    place = pl.ds(asked_ref[owner * LANES + slot], 1)
                    term = slope_ref[owner * LANES + slot] * wide[pl.ds(owner * LANES + slot, 1), :]
                    one[place, :] = one[place, :] + term
            return j + 1

        def more(j):
            at = jnp.minimum(j * unroll, LANES - 1)
            first = asked_ref[s * LANES + at]
            for k in range(1, 4):
                first = jnp.minimum(first, asked_ref[(k * each + s) * LANES + at])
            return jnp.logical_and(j * unroll < LANES, first < DUMP)

        lax.while_loop(more, group, 0)
        return carry

    lax.fori_loop(0, each, source, 0)
    total = (a0[0:ROWS, :] + a1[0:ROWS, :]) + (a2[0:ROWS, :] + a3[0:ROWS, :])
    out_ref[...] = total


def body(entity_table, relation_table, head_row, relation_id, tail_owner, tail_row, negative_row):
    negatives = negative_row.shape[1]
    negs = negative_row.reshape(CHIPS * negatives)
    wide = pltpu.VMEM((ROWS + 8, LANES), F32)
    lists = (BUCKETS, 1, LANES)
    blocks = (EDGES // LANES, 1, LANES)
    grid = (BUCKETS, LANES, LANES)
    half = pltpu.VMEM((SPAN // 2, NEG_PAD), F32)
    packs = pltpu.VMEM((CHIPS, NEG_PAD + SPAN, LANES), BF16)
    flag = pltpu.SemaphoreType.DMA
    flat32 = pltpu.VMEM((EDGES, LANES), F32)
    asked, came, slopes, loss, head_grad, rel_grad, neg_grad = call(
        functools.partial(forward_kernel, negatives), "forward",
        (shape(lists, jnp.int32), shape(grid, BF16), shape(lists, F32), shape(blocks, F32),
         shape((EDGES, LANES), F32), shape((EDGES, LANES), F32),
         shape((CHIPS, NEG_PAD, LANES), F32)),
        [SM] * 3 + [VM] * 4,
        [wide, pltpu.VMEM((RELS, LANES), F32), pltpu.VMEM((EDGES + 8, LANES), F32),
         flat32, flat32, flat32, flat32,
         pltpu.VMEM((COLS, SPAN // 2, NEG_PAD), BF16),
         pltpu.VMEM((BUCKETS * LANES, LANES), F32), pltpu.VMEM(blocks, jnp.int32),
         pltpu.VMEM(lists, jnp.int32), pltpu.VMEM(lists, jnp.int32),
         pltpu.VMEM(grid, BF16), pltpu.VMEM(grid, BF16), pltpu.VMEM(grid, BF16),
         packs, packs, half, half, half,
         pltpu.VMEM((COLS,) + blocks, F32), pltpu.VMEM((COLS, 2, SPAN // 2), F32),
         pltpu.VMEM(lists, F32), pltpu.VMEM(blocks, F32), pltpu.VMEM(blocks, F32),
         pltpu.SMEM(lists, jnp.int32),
         pltpu.SMEM(blocks, jnp.int32), pltpu.SMEM(lists, jnp.int32),
         flag((3,)), flag((4,)), flag((4,)), flag((CHIPS,)), flag((CHIPS,)), flag((2,)),
         flag((2,)), flag((2 * CHIPS,)), flag((2 * CHIPS,)), flag((2 * CHIPS,)),
         flag((2 * CHIPS,)), flag((2,)), flag((2,))],
        flops=600000000, size=40000000, group=0,
    )(head_row, relation_id, negs, tail_owner.reshape(1, EDGES), tail_row.reshape(1, EDGES),
      entity_table, relation_table)

    rel_local = call(
        functools.partial(relation_kernel, 16), "relations", shape((RELS, LANES), BF16),
        [SM, VM], [pltpu.VMEM((RELS, LANES), F32)] * 4, size=10000000,
    )(relation_id, rel_grad)
    rel_parts = lax.all_to_all(rel_local.reshape(BUCKETS, LANES, LANES), "bucket",
                               split_axis=0, concat_axis=0, tiled=True)
    grad = call(
        functools.partial(entity_kernel, 8, negatives), "entities", shape((ROWS, LANES), F32),
        [SM] * 4 + [VM] * 3,
        [pltpu.VMEM((BUCKETS * LANES, LANES), F32)] + [wide] * 4, size=60000000,
    )(head_row, negs, asked.reshape(BUCKETS * LANES), slopes.reshape(BUCKETS * LANES), head_grad,
      neg_grad, came.reshape(BUCKETS * LANES, LANES))
    relation_grad = jnp.sum(rel_parts.astype(F32), axis=0)
    return (loss.reshape(EDGES), grad, relation_grad)


def solution(mesh):
    in_specs = (
        P("bucket", "col"),
        P(None, "col"),
        P("bucket"),
        P("bucket"),
        P("bucket", None),
        P("bucket"),
        P("bucket", None),
    )
    out_specs = (P("bucket"), P("bucket", "col"), P("bucket", "col"))
    return jax.shard_map(body, mesh=mesh, in_specs=in_specs, out_specs=out_specs, check_vma=False)
```
